256 devices in a mesh: key: 128 (over y, z, x), feat: 2 (over core).
Axes of the slice: x: 4, y: 4, z: 8, core: 2. Of those that a mesh axis runs over, the one named last changes fastest.
Arguments:
- partials: bfloat16 [8192, 64, 384], P('key', 'feat'), may hold values from -6 to 6
- dest_key: int32 [8192], P('key'), may hold values from 0 to 16383, as said below
- active_from: int32 [16384], P('key'), may hold values from 0 to 383
- cohort: int32 [16384], P('key'), may hold values from 0 to 15, as said below
- decay_rate: float32 [3, 64], P(None, 'feat'), may hold values from 0.01 to 0.7
Outputs:
- windowed: bfloat16 [16384, 3, 64, 384], P('key', None, 'feat')
- cohort_mean: float32 [16, 3, 64, 384], P(None, None, 'feat', 'key')
The draws below stay inside these ranges and needn't reach their ends.
Inputs may be any that keep to these rules, and one draw needn't show every extreme that they name: `dest_key`: owner of key k is k // 128. The 64 rows of one device name at most one key of any one owner; in every draw some owner gets exactly 1 row from every device. Cohort sizes are uneven, and a cohort may have no keys.
All inputs are finite; a program needn't handle non-finite values.
Results may differ from the reference program's by a relative error of at most 0.012.
Values may be sent and summed in bfloat16 or wider, within the bound.
A program may use at most 192 MiB of HBM per device.

```python
import math
import jax
import jax.numpy as jnp
from jax import lax

KEYS_DEV = 128
CAP = 1
FEAT = 64
DAYS = 384
BLOCK = 128
WIN_A = 7
WIN_B = 28
WIN_C = 91
COHORTS = 16
KEYS = 16384
ROWS_DEV = 64
ROWS = 8192


def draw_dest_key(key, part):
    key = jax.random.fold_in(key, 11)
    sources = KEYS // KEYS_DEV
    hot_owner = jax.random.randint(jax.random.fold_in(key, 1), (), 0, sources)

    def per_source(source):
        sub_key = jax.random.fold_in(key, source + 2)
        slot_all = jnp.arange(sources * CAP)
        owner_of = slot_all // CAP
        order = jax.random.permutation(jax.random.fold_in(sub_key, 0), sources * CAP)
        forced = (owner_of == hot_owner) | (owner_of == (source + 1) % sources)
        score = jnp.where(forced, -1 - slot_all, order)
        chosen = jnp.argsort(score, stable=True)[:ROWS_DEV]
        owners = chosen // CAP
        first_pick = jax.random.randint(jax.random.fold_in(sub_key, 1), (ROWS_DEV,), 0, KEYS_DEV)
        second_pick = jax.random.randint(jax.random.fold_in(sub_key, 2), (ROWS_DEV,), 0, KEYS_DEV)
        target = owners * KEYS_DEV + jnp.minimum(first_pick, second_pick)
        return target[jax.random.permutation(jax.random.fold_in(sub_key, 3), ROWS_DEV)]
    return jax.vmap(per_source)(jnp.arange(sources)).reshape(-1).astype(jnp.int32)


def draw_cohort(key, part):
    key = jax.random.fold_in(key, 23)
    used_count = COHORTS - 1
    first_pick = jax.random.randint(jax.random.fold_in(key, 1), (KEYS,), 0, used_count)
    second_pick = jax.random.randint(jax.random.fold_in(key, 2), (KEYS,), 0, used_count)
    labels = jax.random.permutation(jax.random.fold_in(key, 3), used_count).astype(jnp.int32)
    picked = labels[jnp.minimum(first_pick, second_pick)]
    empty_cohort = jax.random.randint(jax.random.fold_in(key, 4), (), 1, COHORTS - 1)
    mapped = picked + (picked >= empty_cohort).astype(jnp.int32)
    low_pos = jax.random.randint(jax.random.fold_in(key, 5), (), 0, KEYS)
    high_pos = (low_pos + 1 + jax.random.randint(jax.random.fold_in(key, 6), (), 0, KEYS - 1)) % KEYS
    positions = jnp.arange(KEYS)
    mapped = jnp.where(positions == low_pos, 0, mapped)
    mapped = jnp.where(positions == high_pos, COHORTS - 1, mapped)
    return mapped.astype(jnp.int32)


def touch_ends(drawn, key, smallest, high):
    extent = drawn.shape
    spot = [jax.random.randint(jax.random.fold_in(key, axis), (), 0, extent[axis]) for axis in range(len(extent))]
    drawn = drawn.at[tuple(spot)].set(smallest)
    longest = extent.index(max(extent))
    spot[longest] = (spot[longest] + 1) % extent[longest]
    return drawn.at[tuple(spot)].set(high)


def levels(stream_key, extent, cuts, least, top_value):
    level, own = 1.0, jax.random.fold_in(stream_key, 6)
    for position, blocks in cuts:
        heights = jnp.exp(jax.random.uniform(jax.random.fold_in(own, position), (blocks,), jnp.float32, least / len(cuts), top_value / len(cuts)))
        level = level * jnp.repeat(heights, extent[position] // blocks).reshape([-1 if axis == position else 1 for axis in range(len(extent))])
    return level


def bell_draw(key, extent, spread, most, cuts=(), held_as=jnp.bfloat16):
    level = levels(key, extent, cuts, -0.22, 0.18) if cuts else 1.0
    entries = jax.random.normal(key, extent, jnp.float32) * spread * level
    return jnp.minimum(jnp.maximum(entries, -most), most).astype(held_as)


def setup_inputs(seed: int = 0) -> dict:
    arg_keys = jax.random.split(jax.random.key(seed), 6)
    partials = bell_draw(arg_keys[0], (ROWS, FEAT, DAYS), 1.0, 6.0, ((0, 128), (1, 2)))
    dest_key = draw_dest_key(jax.random.fold_in(arg_keys[5], 71), 0)
    active_from = touch_ends(jax.random.randint(arg_keys[2], (KEYS,), 0, DAYS), jax.random.fold_in(arg_keys[2], 1), 0, DAYS - 1).astype(jnp.int32)
    cohort = draw_cohort(jax.random.fold_in(arg_keys[5], 71), 0)
    decay_rate = jnp.clip(jnp.exp(math.log(0.7) - 4.248495 * jax.random.uniform(arg_keys[4], (3, FEAT), jnp.float32) ** levels(arg_keys[4], (3, FEAT), ((1, 2),), -0.2, 0.2)), 0.01, 0.7)
    return {"partials": partials, "dest_key": dest_key, "active_from": active_from, "cohort": cohort, "decay_rate": decay_rate}


def band_table(decay_rates):
    source_day = jnp.arange(2 * BLOCK)[:, None]
    target_day = jnp.arange(BLOCK)[None, :]
    lag_days = (BLOCK + target_day - source_day).astype(jnp.float32)
    columns = []
    for window_idx, window_len in enumerate((WIN_A, WIN_B, WIN_C)):
        in_band = (lag_days >= 0) & (lag_days < window_len)
        weights = jnp.exp(-decay_rates[window_idx][:, None, None] * lag_days[None])
        columns.append(jnp.where(in_band[None], weights, 0.0))
    return jnp.concatenate(columns, axis=2).astype(jnp.bfloat16)

def reference(partials, dest_key, active_from, cohort, decay_rate):
    band_weights = band_table(decay_rate)
    live_mask = (jnp.arange(DAYS)[None, :] >= active_from[:, None]).astype(jnp.float32)
    blocks = DAYS // BLOCK

    def one_feature(inputs):
        feature_idx, weights = inputs
        column = lax.dynamic_index_in_dim(partials, feature_idx, 1, keepdims=False).astype(jnp.float32)
        daily = (jax.ops.segment_sum(column, dest_key, num_segments=KEYS) * live_mask).astype(jnp.bfloat16)
        padded = jnp.concatenate([jnp.zeros((KEYS, BLOCK), jnp.bfloat16), daily], axis=1)
        outputs = []
        for block_idx in range(blocks):
            piece = padded[:, block_idx * BLOCK:block_idx * BLOCK + 2 * BLOCK]
            outputs.append(jnp.dot(piece, weights, preferred_element_type=jnp.float32))
        stacked = jnp.stack(outputs, axis=1).reshape(KEYS, blocks, 3, BLOCK)
        raw_window = stacked.transpose(0, 2, 1, 3).reshape(KEYS, 3, DAYS).astype(jnp.bfloat16)
        squares = lax.optimization_barrier(jnp.sum(jnp.square(raw_window.astype(jnp.float32)), axis=2))
        return (raw_window, squares)
    raw_all, square_all = lax.map(one_feature, (jnp.arange(FEAT).astype(jnp.int32), band_weights))
    norm_scale = lax.rsqrt(lax.optimization_barrier(jnp.sum(square_all, axis=0)) / (FEAT * DAYS) + 1e-05)

    def normalize(raw_window):
        return (raw_window.astype(jnp.float32) * norm_scale[:, :, None]).astype(jnp.bfloat16)
    windowed = lax.map(normalize, raw_all).transpose(1, 2, 0, 3)
    member = cohort[None, :] == jnp.arange(COHORTS)[:, None]
    cohort_sum = jnp.dot(member.astype(jnp.bfloat16), windowed.reshape(KEYS, -1), preferred_element_type=jnp.float32)
    cohort_count = lax.optimization_barrier(jnp.sum(member.astype(jnp.float32), axis=1))
    cohort_mean = cohort_sum.reshape(COHORTS, 3, FEAT, DAYS) / jnp.maximum(cohort_count, 1.0)[:, None, None, None]
    return (windowed, cohort_mean)
```

```python
import functools

import jax
import jax.numpy as jnp
from jax import lax
from jax.experimental import pallas as pl
from jax.experimental.pallas import tpu as pltpu
from jax.sharding import PartitionSpec as P

CAP = 1
FEAT = 64
BLOCK = 128
WIN_A = 7
WIN_B = 28
WIN_C = 91
COHORTS = 16
NY, NZ, NX = 4, 8, 4
MESH = pl.DeviceIdType.MESH


def band_table(decay_rates):
    source_day = jnp.arange(2 * BLOCK)[:, None]
    target_day = jnp.arange(BLOCK)[None, :]
    lag_days = (BLOCK + target_day - source_day).astype(jnp.float32)
    columns = []
    for window_idx, window_len in enumerate((WIN_A, WIN_B, WIN_C)):
        in_band = (lag_days >= 0) & (lag_days < window_len)
        weights = jnp.exp(-decay_rates[window_idx][:, None, None] * lag_days[None])
        columns.append(jnp.where(in_band[None], weights, 0.0))
    return jnp.concatenate(columns, axis=2).astype(jnp.bfloat16)


def peer_at(me, step):
    y, z, x = me // (NZ * NX), (me // NX) % NZ, me % NX
    dy, dz, dx = step // (NZ * NX), (step // NX) % NZ, step % NX
    return ((y + dy) % NY) * (NZ * NX) + ((z + dz) % NZ) * NX + (x + dx) % NX


def exchange_kernel(peers, rows_ref, slot_ref, out_ref, held, packed, send_sem, recv_sem, own_sem):
    me = lax.axis_index("key")
    load = pltpu.make_async_copy(rows_ref, held, own_sem)
    load.start()
    barrier = pltpu.get_barrier_semaphore()

    def greet(step, carry):
        pl.semaphore_signal(barrier, 1, device_id={"key": peer_at(me, step)}, device_id_type=MESH)
        return carry

    lax.fori_loop(1, peers, greet, 0)
    load.wait()
    packed[0] = held[slot_ref[me]]
    own = pltpu.make_async_copy(packed.at[0], out_ref.at[me], own_sem)
    own.start()
    pl.semaphore_wait(barrier, peers - 1)

    def send(step, carry):
        peer = peer_at(me, step)
        packed[step] = held[slot_ref[peer]]
        pltpu.make_async_remote_copy(
            src_ref=packed.at[step],
            dst_ref=out_ref.at[me],
            send_sem=send_sem,
            recv_sem=recv_sem,
            device_id={"key": peer},
            device_id_type=MESH,
        ).start()
        return carry

    lax.fori_loop(1, peers, send, 0)
    own.wait()
    whole = pltpu.make_async_remote_copy(
        src_ref=packed.at[pl.ds(1, peers - 1)],
        dst_ref=out_ref.at[pl.ds(0, peers - 1)],
        send_sem=send_sem,
        recv_sem=recv_sem,
        device_id={"key": peer_at(me, 1)},
        device_id_type=MESH,
    )
    whole.wait_send()
    whole.wait_recv()


def exchange(partials, slot_row, peers):
    rows, feats, days = partials.shape
    return pl.pallas_call(
        functools.partial(exchange_kernel, peers),
        out_shape=jax.ShapeDtypeStruct((peers, feats, days), partials.dtype),
        in_specs=[
            pl.BlockSpec(memory_space=pl.ANY),
            pl.BlockSpec(memory_space=pltpu.SMEM),
        ],
        out_specs=pl.BlockSpec(memory_space=pl.ANY),
        scratch_shapes=[
            pltpu.VMEM((rows, feats, days), partials.dtype),
            pltpu.VMEM((peers, feats, days), partials.dtype),
            pltpu.SemaphoreType.DMA,
            pltpu.SemaphoreType.DMA,
            pltpu.SemaphoreType.DMA,
        ],
        compiler_params=pltpu.CompilerParams(
            collective_id=0, has_side_effects=True, vmem_limit_bytes=32 << 20
        ),
        cost_estimate=pl.CostEstimate(flops=0, bytes_accessed=200_000_000, transcendentals=0),
    )(partials, slot_row)


def on_device(partials, dest_key, active_from, cohort, decay_rate):
    key_devs = lax.axis_size("key")
    row_count, feat_count, day_count = partials.shape
    key_count = active_from.shape[0]
    me = lax.axis_index("key")
    owner_dev = dest_key // key_count
    match = owner_dev[None, :] == jnp.arange(key_devs)[:, None]
    slot_row = jnp.sum(jnp.where(match, jnp.arange(row_count)[None, :], 0), axis=1).astype(jnp.int32)
    all_dest = lax.all_gather(dest_key, "key")
    rows = exchange(partials, slot_row, key_devs)
    mine = (all_dest // key_count) == me
    arrived = jnp.sum(jnp.where(mine, all_dest % key_count + 1, 0), axis=1) - 1
    receive = (arrived[None, :] == jnp.arange(key_count)[:, None]).astype(jnp.bfloat16)
    live_mask = (jnp.arange(day_count)[None, :] >= active_from[:, None]).astype(jnp.float32)
    items = rows.shape[1]
    summed = jnp.dot(receive, rows.reshape(rows.shape[0], -1), preferred_element_type=jnp.float32)
    summed = summed.reshape(key_count, items, day_count)
    daily = (summed * live_mask[:, None, :]).astype(jnp.bfloat16)
    band_weights = band_table(decay_rate)
    blocks = day_count // BLOCK
    padded = jnp.concatenate(
        [jnp.zeros((key_count, feat_count, BLOCK), jnp.bfloat16), daily], axis=2
    )
    pieces = jnp.stack(
        [
            padded[:, :, block_idx * BLOCK : block_idx * BLOCK + 2 * BLOCK]
            for block_idx in range(blocks)
        ],
        axis=2,
    )
    raw_window = jnp.einsum(
        "kfji,fio->kfjo", pieces, band_weights, preferred_element_type=jnp.float32
    )
    raw_window = raw_window.reshape(key_count, feat_count, blocks, 3, BLOCK).transpose(
        0, 3, 1, 2, 4
    )
    raw_window = raw_window.reshape(key_count, 3, feat_count, day_count).astype(jnp.bfloat16)
    raw_float = raw_window.astype(jnp.float32)
    squares = jnp.sum(jnp.square(raw_float), axis=(2, 3))
    key_total = lax.psum(squares, "feat")
    norm_scale = lax.rsqrt(key_total / (FEAT * day_count) + 1e-05)
    windowed = (raw_float * norm_scale[:, :, None, None]).astype(jnp.bfloat16)
    member = cohort[None, :] == jnp.arange(COHORTS)[:, None]
    part_table = jnp.dot(
        member.astype(jnp.bfloat16),
        windowed.reshape(key_count, -1),
        preferred_element_type=jnp.float32,
    )
    part_table = part_table.reshape(COHORTS * 3 * feat_count, day_count)
    part_count = jnp.sum(member.astype(jnp.float32), axis=1)
    whole_count = lax.psum(part_count, "key")
    own_days = lax.psum_scatter(part_table.T, "key", scatter_dimension=0, tiled=True)
    day_share = day_count // key_devs
    own_days = own_days.T.reshape(COHORTS, 3, feat_count, day_share)
    cohort_mean = own_days / jnp.maximum(whole_count, 1.0)[:, None, None, None]
    return (windowed, cohort_mean)


def solution(mesh):
    placed = (P("key", "feat", None), P("key"), P("key"), P("key"), P(None, "feat"))
    return jax.shard_map(
        on_device,
        mesh=mesh,
        in_specs=placed,
        out_specs=(P("key", None, "feat", None), P(None, None, "feat", "key")),
        check_vma=False,
    )
```

```python
import functools

import jax
import jax.numpy as jnp
from jax import lax
from jax.experimental import pallas as pl
from jax.experimental.pallas import tpu as pltpu
from jax.sharding import PartitionSpec as P

FEAT = 64
BLOCK = 128
WINDOWS = (7, 28, 91)
COHORTS = 16
NY, NZ, NX = 4, 8, 4
PLANE = NY * NX
MESH = pl.DeviceIdType.MESH


def peer_at(me, step):
    y, z, x = me // (NZ * NX), (me // NX) % NZ, me % NX
    dy, dz, dx = step // (NZ * NX), (step // NX) % NZ, step % NX
    return ((y + dy) % NY) * (NZ * NX) + ((z + dz) % NZ) * NX + (x + dx) % NX


def exchange_kernel(
    peers, rows_ref, slot_ref, note_ref, out_ref, got_ref, held, packed, sems
):
    me = lax.axis_index("key")
    load = pltpu.make_async_copy(rows_ref, held, sems.at[0])
    load.start()
    barrier = pltpu.get_barrier_semaphore()

    def greet(step, carry):
        pl.semaphore_signal(barrier, 1, device_id={"key": peer_at(me, step)}, device_id_type=MESH)
        return carry

    lax.fori_loop(1, peers, greet, 0)
    load.wait()
    packed[0] = held[slot_ref[me]]
    own = pltpu.make_async_copy(packed.at[0], out_ref.at[me], sems.at[0])
    own.start()
    own_note = pltpu.make_async_copy(note_ref.at[me], got_ref.at[me], sems.at[5])
    own_note.start()
    pl.semaphore_wait(barrier, peers - 1)

    def send(step, carry):
        peer = peer_at(me, step)
        packed[step] = held[slot_ref[peer]]
        pltpu.make_async_remote_copy(
            src_ref=packed.at[step],
            dst_ref=out_ref.at[me],
            send_sem=sems.at[1],
            recv_sem=sems.at[2],
            device_id={"key": peer},
            device_id_type=MESH,
        ).start()
        pltpu.make_async_remote_copy(
            src_ref=note_ref.at[peer],
            dst_ref=got_ref.at[me],
            send_sem=sems.at[3],
            recv_sem=sems.at[4],
            device_id={"key": peer},
            device_id_type=MESH,
        ).start()
        return carry

    lax.fori_loop(1, peers, send, 0)
    own.wait()
    own_note.wait()
    others = pl.ds(0, peers - 1)
    for source, target, first in ((packed, out_ref, 1), (note_ref, got_ref, 3)):
        whole = pltpu.make_async_remote_copy(
            src_ref=source.at[others],
            dst_ref=target.at[others],
            send_sem=sems.at[first],
            recv_sem=sems.at[first + 1],
            device_id={"key": peer_at(me, 1)},
            device_id_type=MESH,
        )
        whole.wait_send()
        whole.wait_recv()


def exchange(partials, slot_row, notes, peers):
    rows, feats, days = partials.shape
    return pl.pallas_call(
        functools.partial(exchange_kernel, peers),
        out_shape=(
            jax.ShapeDtypeStruct((peers, feats, days), partials.dtype),
            jax.ShapeDtypeStruct(notes.shape, notes.dtype),
        ),
        in_specs=[
            pl.BlockSpec(memory_space=pl.ANY),
            pl.BlockSpec(memory_space=pltpu.SMEM),
            pl.BlockSpec(memory_space=pltpu.VMEM),
        ],
        out_specs=(pl.BlockSpec(memory_space=pl.ANY), pl.BlockSpec(memory_space=pl.ANY)),
        scratch_shapes=[
            pltpu.VMEM((rows, feats, days), partials.dtype),
            pltpu.VMEM((peers, feats, days), partials.dtype),
            pltpu.SemaphoreType.DMA((6,)),
        ],
        compiler_params=pltpu.CompilerParams(
            collective_id=0, has_side_effects=True, vmem_limit_bytes=32 << 20
        ),
        cost_estimate=pl.CostEstimate(flops=0, bytes_accessed=200_000_000, transcendentals=0),
    )(partials, slot_row, notes)


def window_kernel(
    feats, group, arrived_ref, rate_ref, rows_ref, start_ref, out_ref, square_ref, daily, raw
):
    keys = start_ref.shape[0]
    days_blocks = daily.shape[0]
    step = pl.program_id(0)

    @pl.when(step == 0)
    def _():
        daily[...] = jnp.zeros_like(daily)
        square_ref[...] = jnp.zeros_like(square_ref)

        def add_row(source, carry):
            key = arrived_ref[source]

            @pl.when(key >= 0)
            def _():
                spot = pl.ds(pl.multiple_of(key * feats, feats), feats)
                for b in range(days_blocks):
                    piece = rows_ref[source, :, b * BLOCK : (b + 1) * BLOCK]
                    daily[b, spot, :] += piece.astype(jnp.float32)

            return carry

        lax.fori_loop(0, rows_ref.shape[0], add_row, 0)

    lane = lax.broadcasted_iota(jnp.int32, (keys, BLOCK), 1)
    lag = (
        BLOCK
        + lax.broadcasted_iota(jnp.int32, (2 * BLOCK, BLOCK), 1)
        - lax.broadcasted_iota(jnp.int32, (2 * BLOCK, BLOCK), 0)
    )
    lag_float = lag.astype(jnp.float32)

    def one_feature(local, carry):
        f = step * group + local
        parts = [jnp.zeros((keys, BLOCK), jnp.bfloat16)]
        for b in range(days_blocks):
            piece = daily[b, pl.ds(f, keys, stride=feats), :]
            live = lane + b * BLOCK >= start_ref[...]
            parts.append(jnp.where(live, piece, 0.0).astype(jnp.bfloat16))
        left = jnp.concatenate(
            [jnp.concatenate(parts[b : b + 2], axis=1) for b in range(days_blocks)], axis=0
        )
        bands = []
        for w, length in enumerate(WINDOWS):
            weights = jnp.exp(-rate_ref[w * feats + f] * lag_float)
            inside = (lag >= 0) & (lag < length)
            bands.append(jnp.where(inside, weights, 0.0).astype(jnp.bfloat16))
        result = jnp.dot(left, jnp.concatenate(bands, axis=1), preferred_element_type=jnp.float32)
        for w in range(len(WINDOWS)):
            total = square_ref[w]
            for b in range(days_blocks):
                piece = result[b * keys : (b + 1) * keys, w * BLOCK : (w + 1) * BLOCK]
                raw[w, b, pl.ds(local, keys, stride=group), :] = piece
                total = total + piece * piece
            square_ref[w] = total
        return carry

    lax.fori_loop(0, group, one_feature, 0)

    def pack(key, carry):
        for w in range(len(WINDOWS)):
            for b in range(days_blocks):
                piece = raw[w, b, pl.ds(pl.multiple_of(key * group, group), group), :]
                out_ref[key, w, :, b * BLOCK : (b + 1) * BLOCK] = piece.astype(jnp.bfloat16)
        return carry

    lax.fori_loop(0, keys, pack, 0)


def windows(rows, arrived, active_from, decay_rate):
    sources, feats, days = rows.shape
    keys = active_from.shape[0]
    group = 16
    blocks = days // BLOCK
    kinds = len(WINDOWS)
    start = jnp.broadcast_to(active_from[:, None], (keys, BLOCK))
    return pl.pallas_call(
        functools.partial(window_kernel, feats, group),
        grid=(feats // group,),
        out_shape=(
            jax.ShapeDtypeStruct((keys, kinds, feats, days), jnp.bfloat16),
            jax.ShapeDtypeStruct((kinds, keys, BLOCK), jnp.float32),
        ),
        in_specs=[
            pl.BlockSpec(memory_space=pltpu.SMEM),
            pl.BlockSpec(memory_space=pltpu.SMEM),
            pl.BlockSpec((sources, feats, days), lambda i: (0, 0, 0)),
            pl.BlockSpec((keys, BLOCK), lambda i: (0, 0)),
        ],
        out_specs=(
            pl.BlockSpec((keys, kinds, group, days), lambda i: (0, 0, i, 0)),
            pl.BlockSpec((kinds, keys, BLOCK), lambda i: (0, 0, 0)),
        ),
        scratch_shapes=[
            pltpu.VMEM((blocks, keys * feats, BLOCK), jnp.float32),
            pltpu.VMEM((kinds, blocks, keys * group, BLOCK), jnp.float32),
        ],
        compiler_params=pltpu.CompilerParams(vmem_limit_bytes=56 << 20),
    )(arrived, decay_rate.reshape(-1), rows, start)


def scale_kernel(feats, block, scale_ref, cohort_ref, raw_ref, order_ref, out_ref, table_ref, total, turned):
    step = pl.program_id(0)
    kinds = len(WINDOWS)

    @pl.when(step == 0)
    def _():
        total[...] = jnp.zeros_like(total)

    for local in range(block):
        key = step * block + local
        first = cohort_ref[key] * (kinds * feats)
        for w in range(kinds):
            value = raw_ref[local, w].astype(jnp.float32) * scale_ref[key * kinds + w]
            value = value.astype(jnp.bfloat16)
            out_ref[local, w] = value
            spot = pl.ds(pl.multiple_of(first + w * feats, feats), feats)
            total[spot, :] += value.astype(jnp.float32)

    @pl.when(step == pl.num_programs(0) - 1)
    def _():
        share = order_ref.shape[0] // PLANE
        for g in range(total.shape[0] // BLOCK):
            rows = total[g * BLOCK : (g + 1) * BLOCK, :].astype(jnp.bfloat16)
            by_day = lax.dot_general(
                order_ref[...], rows, (((1,), (1,)), ((), ())), preferred_element_type=jnp.float32
            )
            turned[:, g * share : (g + 1) * share, :] = by_day.reshape(PLANE, share, BLOCK)
        table_ref[...] = turned[...].astype(jnp.bfloat16)


def scale_and_sum(raw, norm_scale, cohort):
    keys, kinds, feats, days = raw.shape
    block = 8
    rows = COHORTS * kinds * feats
    share = days // (NY * NZ * NX)
    place = jnp.arange(days)
    y, x, t, z = place // (days // NY), (place // (share * NZ)) % NX, (place // NZ) % share, place % NZ
    source = ((y * NZ + z) * NX + x) * share + t
    order = (source[:, None] == jnp.arange(days)[None, :]).astype(jnp.bfloat16)
    block_rows = rows // BLOCK * (days // PLANE)
    whole = lambda i: (i, 0, 0, 0)
    return pl.pallas_call(
        functools.partial(scale_kernel, feats, block),
        grid=(keys // block,),
        out_shape=(
            jax.ShapeDtypeStruct(raw.shape, jnp.bfloat16),
            jax.ShapeDtypeStruct((PLANE, block_rows, BLOCK), jnp.bfloat16),
        ),
        in_specs=[
            pl.BlockSpec(memory_space=pltpu.SMEM),
            pl.BlockSpec(memory_space=pltpu.SMEM),
            pl.BlockSpec((block, kinds, feats, days), whole),
            pl.BlockSpec((days, days), lambda i: (0, 0)),
        ],
        out_specs=(
            pl.BlockSpec((block, kinds, feats, days), whole),
            pl.BlockSpec((PLANE, block_rows, BLOCK), lambda i: (0, 0, 0)),
        ),
        scratch_shapes=[
            pltpu.VMEM((rows, days), jnp.float32),
            pltpu.VMEM((PLANE, block_rows, BLOCK), jnp.float32),
        ],
        compiler_params=pltpu.CompilerParams(vmem_limit_bytes=48 << 20),
    )(norm_scale.reshape(-1), cohort, raw, order)


def scatter_kernel(table_ref, out_ref, landed, sums, piece, piece_landed, sems):
    me = lax.axis_index("key")
    y, z, x = me // (NZ * NX), (me // NX) % NZ, me % NX
    barrier = pltpu.get_barrier_semaphore()

    def plane_peer(step):
        ty, tx = (y + step // NX) % NY, (x + step % NX) % NX
        return (ty * NZ + z) * NX + tx, ty * NX + tx

    def line_peer(step):
        tz = (z + step) % NZ
        return (y * NZ + tz) * NX + x, tz

    for step in range(1, PLANE):
        pl.semaphore_signal(barrier, 1, device_id={"key": plane_peer(step)[0]}, device_id_type=MESH)
    for step in range(1, NZ):
        pl.semaphore_signal(barrier, 1, device_id={"key": line_peer(step)[0]}, device_id_type=MESH)
    pl.semaphore_wait(barrier, PLANE - 1 + NZ - 1)

    def send(source, target, step, peer, sem):
        copy = pltpu.make_async_remote_copy(
            src_ref=source,
            dst_ref=target.at[step],
            send_sem=sems.at[0, sem + step],
            recv_sem=sems.at[1, sem + step],
            device_id={"key": peer},
            device_id_type=MESH,
        )
        copy.start()
        return copy

    copies = []
    for step in range(1, PLANE):
        peer, block = plane_peer(step)
        copies.append(send(table_ref.at[block], landed, step, peer, 0))
    for copy in copies:
        copy.wait()
    total = table_ref[y * NX + x].astype(jnp.float32)
    for step in range(1, PLANE):
        total = total + landed[step].astype(jnp.float32)
    sums[...] = total
    count = out_ref.shape[0]
    for tz in range(NZ):
        piece[tz, :count] = sums[pl.ds(tz, count, stride=NZ), :]
    copies = []
    for step in range(1, NZ):
        peer, block = line_peer(step)
        copies.append(send(piece.at[block], piece_landed, step, peer, PLANE))
    for copy in copies:
        copy.wait()
    total = piece[z, :count]
    for step in range(1, NZ):
        total = total + piece_landed[step, :count]
    out_ref[...] = total


def scatter(table):
    _, rows, lanes = table.shape
    own = rows // NZ
    padded = -(-own // 8) * 8
    return pl.pallas_call(
        scatter_kernel,
        out_shape=jax.ShapeDtypeStruct((own, lanes), jnp.float32),
        in_specs=[pl.BlockSpec(memory_space=pltpu.VMEM)],
        out_specs=pl.BlockSpec(memory_space=pltpu.VMEM),
        scratch_shapes=[
            pltpu.VMEM((PLANE, rows, lanes), jnp.bfloat16),
            pltpu.VMEM((rows, lanes), jnp.float32),
            pltpu.VMEM((NZ, padded, lanes), jnp.float32),
            pltpu.VMEM((NZ, padded, lanes), jnp.float32),
            pltpu.SemaphoreType.DMA((2, PLANE + NZ)),
        ],
        compiler_params=pltpu.CompilerParams(
            collective_id=1, has_side_effects=True, vmem_limit_bytes=16 << 20
        ),
    )(table)


def on_device(partials, dest_key, active_from, cohort, decay_rate):
    key_devs = lax.axis_size("key")
    row_count, feat_count, day_count = partials.shape
    key_count = active_from.shape[0]
    kinds = len(WINDOWS)
    match = (dest_key // key_count)[None, :] == jnp.arange(key_devs)[:, None]
    slot_row = jnp.sum(jnp.where(match, jnp.arange(row_count)[None, :], 0), axis=1)
    slot_key = jnp.sum(jnp.where(match, (dest_key % key_count + 1)[None, :], 0), axis=1) - 1
    lane = jnp.arange(BLOCK)
    member = cohort[:, None] == lane[None, :]
    part_count = jnp.sum(member.astype(jnp.int32), axis=0)
    notes = jnp.where(lane[None, :] < COHORTS, part_count[None, :], slot_key[:, None])
    notes = notes.astype(jnp.int32).reshape(key_devs, 1, BLOCK)
    rows, got = exchange(partials, slot_row.astype(jnp.int32), notes, key_devs)
    got = got.reshape(key_devs, BLOCK)
    arrived = got[:, COHORTS]
    whole_count = jnp.sum(got[:, :COHORTS], axis=0).astype(jnp.float32)
    raw, squares = windows(rows, arrived, active_from, decay_rate)
    key_total = lax.psum(jnp.sum(squares, axis=2), "feat")
    norm_scale = lax.rsqrt(key_total.T / (FEAT * day_count) + 1e-05)
    windowed, table = scale_and_sum(raw, norm_scale, cohort)
    own = scatter(table)
    share = day_count // key_devs
    own = own.reshape(-1, share, BLOCK).transpose(0, 2, 1)
    own = own.reshape(COHORTS, kinds, feat_count, share)
    cohort_mean = own / jnp.maximum(whole_count, 1.0)[:, None, None, None]
    return (windowed, cohort_mean)


def solution(mesh):
    placed = (P("key", "feat", None), P("key"), P("key"), P("key"), P(None, "feat"))
    return jax.shard_map(
        on_device,
        mesh=mesh,
        in_specs=placed,
        out_specs=(P("key", None, "feat", None), P(None, None, "feat", "key")),
        check_vma=False,
    )
```

```python
import functools

import jax
import jax.numpy as jnp
from jax import lax
from jax.experimental import pallas as pl
from jax.experimental.pallas import tpu as pltpu
from jax.sharding import PartitionSpec as P

FEAT = 64
BLOCK = 128
WINDOWS = (7, 28, 91)
COHORTS = 16
NY, NZ, NX = 4, 8, 4
PLANE = NY * NX
MESH = pl.DeviceIdType.MESH


DAY_PARTS = 3


def peer_at(me, step):
    y, z, x = me // (NZ * NX), (me // NX) % NZ, me % NX
    dy, dz, dx = step // (NZ * NX), (step // NX) % NZ, step % NX
    return ((y + dy) % NY) * (NZ * NX) + ((z + dz) % NZ) * NX + (x + dx) % NX


def send_to(source, target, send_sem, recv_sem, where):
    copy = pltpu.make_async_remote_copy(
        src_ref=source,
        dst_ref=target,
        send_sem=send_sem,
        recv_sem=recv_sem,
        device_id=where,
        device_id_type=MESH,
    )
    copy.start()
    return copy


def main_kernel(
    slot_ref,
    rate_ref,
    rows_ref,
    note_ref,
    start_ref,
    cohort_ref,
    order_ref,
    raw_ref,
    norm_ref,
    mean_ref,
    held,
    packed,
    landed,
    note_landed,
    wide,
    bands,
    before,
    kept,
    spread,
    staged,
    squares,
    share_out,
    share_in,
    table,
    turned,
    block_out,
    block_in,
    sums,
    piece_out,
    piece_in,
    load_sem,
    send_sems,
    recv_sems,
    pair_sems,
    out_sems,
    block_sems,
    piece_sems,
):
    me = lax.axis_index("key")
    other = {"feat": 1 - lax.axis_index("feat")}
    y, z, x = me // (NZ * NX), (me // NX) % NZ, me % NX
    peers, feats, _ = landed.shape[1:]
    keys = start_ref.shape[1]
    kinds = len(WINDOWS)
    load = pltpu.make_async_copy(rows_ref, held, load_sem)
    load.start()
    barrier = pltpu.get_barrier_semaphore()

    def greet(step, carry):
        pl.semaphore_signal(barrier, 1, device_id={"key": peer_at(me, step)}, device_id_type=MESH)
        return carry

    lax.fori_loop(1, peers, greet, 0)
    pl.semaphore_signal(barrier, 1, device_id=other, device_id_type=MESH)
    load.wait()
    pl.semaphore_wait(barrier, peers)

    for part in range(DAY_PARTS):
        days = slice(part * BLOCK, (part + 1) * BLOCK)

        def send(step, carry):
            peer = peer_at(me, step)
            packed[part, step] = held[slot_ref[peer], :, days]
            where = {"key": peer}
            send_to(packed.at[part, step], landed.at[part, me], send_sems.at[part], recv_sems.at[part], where)
            if part == 0:
                send_to(note_ref.at[peer], note_landed.at[me], send_sems.at[DAY_PARTS], recv_sems.at[DAY_PARTS], where)
            return carry

        lax.fori_loop(1, peers, send, 0)
        landed[part, me] = held[slot_ref[me], :, days]
    note_landed[me] = note_ref[me]

    shape = (2 * BLOCK, BLOCK)
    lag = BLOCK + lax.broadcasted_iota(jnp.int32, shape, 1) - lax.broadcasted_iota(jnp.int32, shape, 0)
    lag_float = lag.astype(jnp.float32)

    def make_band(f, carry):
        for w, length in enumerate(WINDOWS):
            weights = jnp.exp(-rate_ref[w, f] * lag_float)
            inside = (lag >= 0) & (lag < length)
            band = jnp.where(inside, weights, 0.0).astype(jnp.bfloat16)
            bands[f, :, w * BLOCK : (w + 1) * BLOCK] = band
        return carry

    lax.fori_loop(0, feats, make_band, 0)

    start = jnp.broadcast_to(start_ref[...].astype(jnp.float32), (keys, BLOCK)).T
    lane = lax.broadcasted_iota(jnp.int32, (keys, BLOCK), 1)
    lane_float = lane.astype(jnp.float32)
    squares[...] = jnp.zeros_like(squares)

    def whole(source, target, index):
        others = pl.ds(0, peers - 1)
        return pltpu.make_async_remote_copy(
            src_ref=source.at[others],
            dst_ref=target.at[others],
            send_sem=send_sems.at[index],
            recv_sem=recv_sems.at[index],
            device_id={"key": peer_at(me, 1)},
            device_id_type=MESH,
        )

    notes = whole(note_ref, note_landed, DAY_PARTS)
    notes.wait_recv()
    arrived = note_landed[:, 0, :BLOCK]
    receive = jnp.where(arrived == lane, 1.0, 0.0).T.astype(jnp.bfloat16)
    count = jnp.sum(note_landed[:, 0, BLOCK:], axis=0, keepdims=True).astype(jnp.float32)

    def pack(part):
        def one_key(key, carry):
            spot = pl.ds(pl.multiple_of(key * feats, feats), feats)
            for w in range(kinds):
                staged[part % 2, key, w] = spread[w, spot, :].astype(jnp.bfloat16)
            return carry

        lax.fori_loop(0, keys, one_key, 0)
        copy = pltpu.make_async_copy(
            staged.at[part % 2],
            raw_ref.at[:, :, :, pl.ds(part * BLOCK, BLOCK)],
            out_sems.at[part],
        )
        copy.start()
        return copy

    writes = []
    for part in range(DAY_PARTS):
        arrival = whole(packed.at[part], landed.at[part], part)
        arrival.wait_recv()

        def widen(source, carry):
            spot = pl.ds(pl.multiple_of(source * feats, feats), feats)
            wide[spot, :] = landed[part, source].astype(jnp.float32)
            return carry

        lax.fori_loop(0, peers, widen, 0)
        live = lane_float + float(part * BLOCK) >= start

        def features(pair, carry):
            columns = []
            for local in range(2):
                f = pair * 2 + local
                columns.append(wide[pl.ds(f, peers, stride=feats), :].astype(jnp.bfloat16))
            summed = jnp.dot(receive, jnp.concatenate(columns, axis=1), preferred_element_type=jnp.float32)
            for local in range(2):
                f = pair * 2 + local
                daily = summed[:, local * BLOCK : (local + 1) * BLOCK]
                daily = jnp.where(live, daily, 0.0).astype(jnp.bfloat16)
                if part == 0:
                    result = jnp.dot(daily, bands[f, BLOCK:, :], preferred_element_type=jnp.float32)
                else:
                    both = jnp.concatenate([before[f], daily], axis=1)
                    result = jnp.dot(both, bands[f], preferred_element_type=jnp.float32)
                if part < DAY_PARTS - 1:
                    before[f] = daily
                kept[f, part] = result.astype(jnp.bfloat16)
                for w in range(kinds):
                    piece = result[:, w * BLOCK : (w + 1) * BLOCK]
                    spread[w, pl.ds(f, keys, stride=feats), :] = piece
                    squares[w] += piece * piece
            return carry

        lax.fori_loop(0, feats // 2, features, 0)
        if part < DAY_PARTS - 1:
            writes.append(pack(part))

    for w in range(kinds):
        share_out[w : w + 1, :] = jnp.sum(squares[w].T, axis=0, keepdims=True)
    share = send_to(share_out, share_in, pair_sems.at[0], pair_sems.at[1], other)
    share.wait()
    mean_square = (share_out[...] + share_in[...]) / (FEAT * DAY_PARTS * BLOCK)
    norm = lax.rsqrt(mean_square + 1e-05)
    norm_ref[...] = norm
    cohort_row = lax.broadcasted_iota(jnp.int32, (COHORTS, keys), 0)
    member = cohort_row == jnp.broadcast_to(cohort_ref[...], (COHORTS, keys))
    weights = [jnp.where(member, norm[w : w + 1, :], 0.0) for w in range(kinds)]
    weights = jnp.concatenate(weights, axis=0)
    high = weights.astype(jnp.bfloat16)
    low = (weights - high.astype(jnp.float32)).astype(jnp.bfloat16)
    weights = jnp.concatenate([high, low], axis=0)

    def add_cohorts(f, carry):
        for part in range(DAY_PARTS):
            result = jnp.dot(weights, kept[f, part], preferred_element_type=jnp.float32)
            for w in range(kinds):
                lanes = slice(w * BLOCK, (w + 1) * BLOCK)
                top = result[w * COHORTS : (w + 1) * COHORTS, lanes]
                rest = result[(kinds + w) * COHORTS : (kinds + w + 1) * COHORTS, lanes]
                spot = pl.ds(pl.multiple_of(f * COHORTS, COHORTS), COHORTS)
                table[w, spot, part * BLOCK : (part + 1) * BLOCK] = top + rest
        return carry

    lax.fori_loop(0, feats, add_cohorts, 0)

    def plane_peer(step):
        ty, tx = (y + step // NX) % NY, (x + step % NX) % NX
        return (ty * NZ + z) * NX + tx, ty * NX + tx

    def line_peer(step):
        tz = (z + step) % NZ
        return (y * NZ + tz) * NX + x, tz

    rows = block_out.shape[2]
    each = order_ref.shape[0] // PLANE
    block_copies = []
    for w in range(kinds):
        for g in range(rows // each):
            lines = table[w, g * BLOCK : (g + 1) * BLOCK, :].astype(jnp.bfloat16)
            by_day = lax.dot_general(
                order_ref[...], lines, (((1,), (1,)), ((), ())), preferred_element_type=jnp.float32
            )
            turned[:, g * each : (g + 1) * each, :] = by_day.reshape(PLANE, each, BLOCK)
        block_out[w] = turned[...].astype(jnp.bfloat16)
        for step in range(1, PLANE):
            peer, block = plane_peer(step)
            sems = block_sems.at[0, w, step], block_sems.at[1, w, step]
            block_copies.append(
                send_to(block_out.at[w, block], block_in.at[w, step], *sems, {"key": peer})
            )
    writes[0].wait()
    last_write = pack(DAY_PARTS - 1)
    for w in range(kinds):
        total = block_out[w, y * NX + x].astype(jnp.float32)
        for step in range(1, PLANE):
            block_copies[w * (PLANE - 1) + step - 1].wait_recv()
            total = total + block_in[w, step].astype(jnp.float32)
        sums[w * rows : (w + 1) * rows, :] = total
    own_rows = mean_ref.shape[0]
    for tz in range(NZ):
        piece_out[tz, :own_rows] = sums[pl.ds(tz, own_rows, stride=NZ), :]
    piece_copies = []
    for step in range(1, NZ):
        peer, block = line_peer(step)
        sems = piece_sems.at[0, step], piece_sems.at[1, step]
        piece_copies.append(send_to(piece_out.at[block], piece_in.at[step], *sems, {"key": peer}))
    total = piece_out[z, :own_rows]
    for step in range(1, NZ):
        piece_copies[step - 1].wait_recv()
        total = total + piece_in[step, :own_rows]
    mean_ref[...] = total / jnp.maximum(count, 1.0)

    for part in range(DAY_PARTS):
        whole(packed.at[part], landed.at[part], part).wait_send()
    notes.wait_send()
    for copy in block_copies + piece_copies:
        copy.wait_send()
    writes[1].wait()
    last_write.wait()


def day_order(days):
    share = days // (NY * NZ * NX)
    place = jnp.arange(days)
    y, x, t, z = place // (days // NY), (place // (share * NZ)) % NX, (place // NZ) % share, place % NZ
    source = ((y * NZ + z) * NX + x) * share + t
    return (source[:, None] == jnp.arange(days)[None, :]).astype(jnp.bfloat16)


def main(partials, slot_row, notes, active_from, cohort, decay_rate):
    rows, feats, days = partials.shape
    peers = slot_row.shape[0]
    keys = active_from.shape[0]
    kinds = len(WINDOWS)
    lines = feats * COHORTS
    block_rows = lines // BLOCK * (days // PLANE)
    own_rows = kinds * block_rows // NZ
    padded = -(-own_rows // 8) * 8
    vmem = pl.BlockSpec(memory_space=pltpu.VMEM)
    smem = pl.BlockSpec(memory_space=pltpu.SMEM)
    hbm = pl.BlockSpec(memory_space=pl.ANY)
    half, full = jnp.bfloat16, jnp.float32
    return pl.pallas_call(
        main_kernel,
        out_shape=(
            jax.ShapeDtypeStruct((keys, kinds, feats, days), half),
            jax.ShapeDtypeStruct((kinds, keys), full),
            jax.ShapeDtypeStruct((own_rows, BLOCK), full),
        ),
        in_specs=[smem, smem, hbm, vmem, vmem, vmem, vmem],
        out_specs=(hbm, vmem, vmem),
        scratch_shapes=[
            pltpu.VMEM((rows, feats, days), half),
            pltpu.VMEM((DAY_PARTS, peers, feats, BLOCK), half),
            pltpu.VMEM((DAY_PARTS, peers, feats, BLOCK), half),
            pltpu.VMEM(notes.shape, notes.dtype),
            pltpu.VMEM((peers * feats, BLOCK), full),
            pltpu.VMEM((feats, 2 * BLOCK, kinds * BLOCK), half),
            pltpu.VMEM((feats, keys, BLOCK), half),
            pltpu.VMEM((feats, DAY_PARTS, keys, kinds * BLOCK), half),
            pltpu.VMEM((kinds, keys * feats, BLOCK), full),
            pltpu.VMEM((2, keys, kinds, feats, BLOCK), half),
            pltpu.VMEM((kinds, keys, BLOCK), full),
            pltpu.VMEM((kinds, keys), full),
            pltpu.VMEM((kinds, keys), full),
            pltpu.VMEM((kinds, lines, days), full),
            pltpu.VMEM((PLANE, block_rows, BLOCK), full),
            pltpu.VMEM((kinds, PLANE, block_rows, BLOCK), half),
            pltpu.VMEM((kinds, PLANE, block_rows, BLOCK), half),
            pltpu.VMEM((kinds * block_rows, BLOCK), full),
            pltpu.VMEM((NZ, padded, BLOCK), full),
            pltpu.VMEM((NZ, padded, BLOCK), full),
            pltpu.SemaphoreType.DMA,
            pltpu.SemaphoreType.DMA((DAY_PARTS + 1,)),
            pltpu.SemaphoreType.DMA((DAY_PARTS + 1,)),
            pltpu.SemaphoreType.DMA((2,)),
            pltpu.SemaphoreType.DMA((DAY_PARTS,)),
            pltpu.SemaphoreType.DMA((2, kinds, PLANE)),
            pltpu.SemaphoreType.DMA((2, NZ)),
        ],
        compiler_params=pltpu.CompilerParams(
            collective_id=0, has_side_effects=True, vmem_limit_bytes=60 << 20
        ),
    )(
        slot_row,
        decay_rate,
        partials,
        notes,
        active_from.reshape(1, keys),
        cohort.reshape(1, keys),
        day_order(days),
    )


def scale_kernel(scale_ref, raw_ref, out_ref):
    block, kinds = raw_ref.shape[:2]
    step = pl.program_id(0)
    for local in range(block):
        for w in range(kinds):
            value = raw_ref[local, w].astype(jnp.float32) * scale_ref[w, step * block + local]
            out_ref[local, w] = value.astype(jnp.bfloat16)


def scale(raw, norm_scale):
    keys, kinds, feats, days = raw.shape
    block = 16
    spec = pl.BlockSpec((block, kinds, feats, days), lambda i: (i, 0, 0, 0))
    return pl.pallas_call(
        scale_kernel,
        grid=(keys // block,),
        out_shape=jax.ShapeDtypeStruct(raw.shape, jnp.bfloat16),
        in_specs=[pl.BlockSpec(memory_space=pltpu.SMEM), spec],
        out_specs=spec,
        compiler_params=pltpu.CompilerParams(vmem_limit_bytes=60 << 20),
    )(norm_scale, raw)


def on_device(partials, dest_key, active_from, cohort, decay_rate):
    key_devs = lax.axis_size("key")
    row_count, feat_count, day_count = partials.shape
    key_count = active_from.shape[0]
    match = (dest_key // key_count)[None, :] == jnp.arange(key_devs)[:, None]
    slot_row = jnp.sum(jnp.where(match, jnp.arange(row_count)[None, :], 0), axis=1)
    slot_key = jnp.sum(jnp.where(match, (dest_key % key_count + 1)[None, :], 0), axis=1) - 1
    lane = jnp.arange(2 * BLOCK)
    member = cohort[:, None] == lane[None, :] % COHORTS
    part_count = jnp.sum(member.astype(jnp.int32), axis=0)
    notes = jnp.where(lane[None, :] < BLOCK, slot_key[:, None], part_count[None, :])
    notes = notes.astype(jnp.int32).reshape(key_devs, 1, 2 * BLOCK)
    slot_row = slot_row.astype(jnp.int32)
    raw, norm_scale, own = main(partials, slot_row, notes, active_from, cohort, decay_rate)
    windowed = scale(raw, norm_scale)
    kinds = len(WINDOWS)
    share = day_count // key_devs
    own = own.reshape(kinds, feat_count * COHORTS // BLOCK, share, BLOCK // COHORTS, COHORTS)
    own = own.transpose(4, 0, 1, 3, 2)
    return (windowed, own.reshape(COHORTS, kinds, feat_count, share))


def solution(mesh):
    placed = (P("key", "feat", None), P("key"), P("key"), P("key"), P(None, "feat"))
    return jax.shard_map(
        on_device,
        mesh=mesh,
        in_specs=placed,
        out_specs=(P("key", None, "feat", None), P(None, None, "feat", "key")),
        check_vma=False,
    )
```

```python
import functools

import jax
import jax.numpy as jnp
import numpy as np
from jax import lax
from jax.experimental import pallas as pl
from jax.experimental.pallas import tpu as pltpu
from jax.sharding import PartitionSpec as P

FEAT = 64
BLOCK = 128
WINDOWS = (7, 28, 91)
COHORTS = 16
NY, NZ, NX = 4, 8, 4
PLANE = NY * NX
MESH = pl.DeviceIdType.MESH


DAY_PARTS = 3
AT_ONCE = 4


def peer_at(me, step):
    y, z, x = me // (NZ * NX), (me // NX) % NZ, me % NX
    dy, dz, dx = step // (NZ * NX), (step // NX) % NZ, step % NX
    return ((y + dy) % NY) * (NZ * NX) + ((z + dz) % NZ) * NX + (x + dx) % NX


def far_first(peers):
    def distance(step):
        place = (step // (NZ * NX), NY), ((step // NX) % NZ, NZ), (step % NX, NX)
        return sum(min(d, n - d) for d, n in place)

    return sorted(range(1, peers), key=lambda step: (-distance(step), step))


def send_to(source, target, send_sem, recv_sem, where):
    copy = pltpu.make_async_remote_copy(
        src_ref=source,
        dst_ref=target,
        send_sem=send_sem,
        recv_sem=recv_sem,
        device_id=where,
        device_id_type=MESH,
    )
    copy.start()
    return copy


def main_kernel(
    rate_ref,
    rows_ref,
    dest_ref,
    start_ref,
    cohort_ref,
    order_ref,
    raw_ref,
    norm_ref,
    mean_ref,
    held,
    slot_row,
    slot_ref,
    note_ref,
    packed,
    landed,
    note_landed,
    wide,
    bands,
    before,
    kept,
    spread,
    staged,
    squares,
    share_out,
    share_in,
    table,
    turned,
    block_out,
    block_in,
    sums,
    piece_out,
    piece_in,
    load_sem,
    send_sems,
    recv_sems,
    pair_sems,
    out_sems,
    block_sems,
    piece_sems,
):
    me = lax.axis_index("key")
    other = {"feat": 1 - lax.axis_index("feat")}
    y, z, x = me // (NZ * NX), (me // NX) % NZ, me % NX
    peers, feats, _ = landed.shape[1:]
    keys = start_ref.shape[1]
    kinds = len(WINDOWS)
    load = pltpu.make_async_copy(rows_ref, held, load_sem)
    load.start()
    barrier = pltpu.get_barrier_semaphore()

    for step in far_first(peers):
        pl.semaphore_signal(barrier, 1, device_id={"key": peer_at(me, step)}, device_id_type=MESH)
    pl.semaphore_signal(barrier, 1, device_id=other, device_id_type=MESH)

    row_count = held.shape[0]
    square = (peers, BLOCK)
    sub = lax.broadcasted_iota(jnp.int32, square, 0)
    lane = lax.broadcasted_iota(jnp.int32, square, 1)

    def down(row):
        return jnp.broadcast_to(row, square).T

    dest = jnp.broadcast_to(dest_ref[...], (peers, row_count)).T
    match = dest // keys == lane[:row_count]
    slot_row[...] = jnp.max(jnp.where(match, sub[:row_count], 0), axis=0, keepdims=True)
    to_scalar = pltpu.make_async_copy(slot_row, slot_ref, pair_sems.at[0])
    to_scalar.start()
    slot_key = jnp.max(jnp.where(match, dest % keys, -1), axis=0, keepdims=True)
    note_ref[:, 0, :BLOCK] = down(slot_key)
    in_cohort = down(cohort_ref[...]) == lane % COHORTS
    part_count = jnp.sum(jnp.where(in_cohort, 1, 0), axis=0, keepdims=True)
    note_ref[:, 0, BLOCK:] = jnp.broadcast_to(part_count, square)
    to_scalar.wait()
    load.wait()
    pl.semaphore_wait(barrier, peers)

    for part in range(DAY_PARTS):
        days = slice(part * BLOCK, (part + 1) * BLOCK)

        def send(step, carry):
            peer = peer_at(me, step)
            packed[part, step] = held[slot_ref[0, peer], :, days]
            where = {"key": peer}
            send_to(packed.at[part, step], landed.at[part, me], send_sems.at[part], recv_sems.at[part], where)
            if part == 0:
                send_to(note_ref.at[peer], note_landed.at[me], send_sems.at[DAY_PARTS], recv_sems.at[DAY_PARTS], where)
            return carry

        lax.fori_loop(1, peers, send, 0)
        landed[part, me] = held[slot_ref[0, me], :, days]
    note_landed[me] = note_ref[me]

    shape = (2 * BLOCK, BLOCK)
    lag = BLOCK + lax.broadcasted_iota(jnp.int32, shape, 1) - lax.broadcasted_iota(jnp.int32, shape, 0)
    lag_float = lag.astype(jnp.float32)

    def make_band(f, carry):
        for w, length in enumerate(WINDOWS):
            weights = jnp.exp(-rate_ref[w, f] * lag_float)
            inside = (lag >= 0) & (lag < length)
            band = jnp.where(inside, weights, 0.0).astype(jnp.bfloat16)
            bands[f, :, w * BLOCK : (w + 1) * BLOCK] = band
        return carry

    lax.fori_loop(0, feats, make_band, 0)

    start = down(start_ref[...])
    squares[...] = jnp.zeros_like(squares)

    def whole(source, target, index):
        others = pl.ds(0, peers - 1)
        return pltpu.make_async_remote_copy(
            src_ref=source.at[others],
            dst_ref=target.at[others],
            send_sem=send_sems.at[index],
            recv_sem=recv_sems.at[index],
            device_id={"key": peer_at(me, 1)},
            device_id_type=MESH,
        )

    notes = whole(note_ref, note_landed, DAY_PARTS)
    notes.wait_recv()
    arrived = note_landed[:, 0, :BLOCK]
    receive = jnp.where(arrived == lane, 1.0, 0.0).T.astype(jnp.bfloat16)
    count = jnp.sum(note_landed[:, 0, BLOCK:], axis=0, keepdims=True).astype(jnp.float32)

    def pack(part):
        def interleave(f, carry):
            for w in range(kinds):
                piece = kept[f, part, :, w * BLOCK : (w + 1) * BLOCK].astype(jnp.float32)
                spread[w, pl.ds(f, keys, stride=feats), :] = piece
            return carry

        lax.fori_loop(0, feats, interleave, 0, unroll=2)

        def some_keys(some, carry):
            for w in range(kinds):
                spot = pl.ds(pl.multiple_of(some * 4 * feats, 4 * feats), 4 * feats)
                piece = spread[w, spot, :].astype(jnp.bfloat16)
                staged[part % 2, pl.ds(some * 4, 4), w] = piece.reshape(4, feats, BLOCK)
            return carry

        lax.fori_loop(0, keys // 4, some_keys, 0)
        copy = pltpu.make_async_copy(
            staged.at[part % 2],
            raw_ref.at[:, :, :, pl.ds(part * BLOCK, BLOCK)],
            out_sems.at[part],
        )
        copy.start()
        return copy

    writes = []
    for part in range(DAY_PARTS):
        arrival = whole(packed.at[part], landed.at[part], part)
        arrival.wait_recv()

        def widen(some, carry):
            spot = pl.ds(pl.multiple_of(some * 8 * feats, 8 * feats), 8 * feats)
            piece = landed[part, pl.ds(some * 8, 8)].astype(jnp.float32)
            wide[spot, :] = piece.reshape(8 * feats, BLOCK)
            return carry

        lax.fori_loop(0, peers // 8, widen, 0)
        live = lane + part * BLOCK >= start

        def features(group, carry):
            columns = []
            for local in range(AT_ONCE):
                f = group * AT_ONCE + local
                columns.append(wide[pl.ds(f, peers, stride=feats), :].astype(jnp.bfloat16))
            summed = jnp.dot(receive, jnp.concatenate(columns, axis=1), preferred_element_type=jnp.float32)
            results = []
            for local in range(AT_ONCE):
                f = group * AT_ONCE + local
                daily = summed[:, local * BLOCK : (local + 1) * BLOCK]
                daily = jnp.where(live, daily, 0.0).astype(jnp.bfloat16)
                if part == 0:
                    result = jnp.dot(daily, bands[f, BLOCK:, :], preferred_element_type=jnp.float32)
                else:
                    both = jnp.concatenate([before[f], daily], axis=1)
                    result = jnp.dot(both, bands[f], preferred_element_type=jnp.float32)
                if part < DAY_PARTS - 1:
                    before[f] = daily
                kept[f, part] = result.astype(jnp.bfloat16)
                results.append(result)
            for w in range(kinds):
                pieces = [result[:, w * BLOCK : (w + 1) * BLOCK] for result in results]
                squares[w] += sum(piece * piece for piece in pieces)
            return carry

        lax.fori_loop(0, feats // AT_ONCE, features, 0)
        if part < DAY_PARTS - 1:
            writes.append(pack(part))

    for w in range(kinds):
        share_out[w : w + 1, :] = jnp.sum(squares[w].T, axis=0, keepdims=True)
    share = send_to(share_out, share_in, pair_sems.at[0], pair_sems.at[1], other)
    share.wait()
    mean_square = (share_out[...] + share_in[...]) / (FEAT * DAY_PARTS * BLOCK)
    norm = lax.rsqrt(mean_square + 1e-05)
    norm_ref[...] = norm
    cohort_row = lax.broadcasted_iota(jnp.int32, (COHORTS, keys), 0)
    member = cohort_row == jnp.broadcast_to(cohort_ref[...], (COHORTS, keys))
    weights = []
    for w in range(kinds):
        scaled = jnp.where(member, norm[w : w + 1, :], 0.0)
        high = scaled.astype(jnp.bfloat16)
        low = (scaled - high.astype(jnp.float32)).astype(jnp.bfloat16)
        weights.append(jnp.concatenate([high, low], axis=0))

    def add_cohorts(group, carry):
        for local in range(AT_ONCE):
            f = group * AT_ONCE + local
            spot = pl.ds(pl.multiple_of(f * COHORTS, COHORTS), COHORTS)
            for part in range(DAY_PARTS):
                for w in range(kinds):
                    lanes = slice(w * BLOCK, (w + 1) * BLOCK)
                    result = jnp.dot(weights[w], kept[f, part, :, lanes], preferred_element_type=jnp.float32)
                    both = result[:COHORTS] + result[COHORTS:]
                    table[w, spot, part * BLOCK : (part + 1) * BLOCK] = both
        return carry

    lax.fori_loop(0, feats // AT_ONCE, add_cohorts, 0)

    def plane_peer(step):
        ty, tx = (y + step // NX) % NY, (x + step % NX) % NX
        return (ty * NZ + z) * NX + tx, ty * NX + tx

    def line_peer(step):
        tz = (z + step) % NZ
        return (y * NZ + tz) * NX + x, tz

    rows = block_out.shape[2]
    each = order_ref.shape[0] // PLANE
    block_copies = []
    for w in range(kinds):
        for g in range(rows // each):
            lines = table[w, g * BLOCK : (g + 1) * BLOCK, :].astype(jnp.bfloat16)
            by_day = lax.dot_general(
                order_ref[...], lines, (((1,), (1,)), ((), ())), preferred_element_type=jnp.float32
            )
            turned[:, g * each : (g + 1) * each, :] = by_day.reshape(PLANE, each, BLOCK)
        block_out[w] = turned[...].astype(jnp.bfloat16)
        for step in range(1, PLANE):
            peer, block = plane_peer(step)
            sems = block_sems.at[0, w, step], block_sems.at[1, w, step]
            block_copies.append(
                send_to(block_out.at[w, block], block_in.at[w, step], *sems, {"key": peer})
            )
    writes[0].wait()
    last_write = pack(DAY_PARTS - 1)
    for w in range(kinds):
        total = block_out[w, y * NX + x].astype(jnp.float32)
        for step in range(1, PLANE):
            block_copies[w * (PLANE - 1) + step - 1].wait_recv()
            total = total + block_in[w, step].astype(jnp.float32)
        sums[w * rows : (w + 1) * rows, :] = total
    own_rows = mean_ref.shape[0]
    for tz in range(NZ):
        piece_out[tz, :own_rows] = sums[pl.ds(tz, own_rows, stride=NZ), :]
    piece_copies = []
    for step in range(1, NZ):
        peer, block = line_peer(step)
        sems = piece_sems.at[0, step], piece_sems.at[1, step]
        piece_copies.append(send_to(piece_out.at[block], piece_in.at[step], *sems, {"key": peer}))
    total = piece_out[z, :own_rows]
    for step in range(1, NZ):
        piece_copies[step - 1].wait_recv()
        total = total + piece_in[step, :own_rows]
    mean_ref[...] = total / jnp.maximum(count, 1.0)

    for part in range(DAY_PARTS):
        whole(packed.at[part], landed.at[part], part).wait_send()
    notes.wait_send()
    for copy in block_copies + piece_copies:
        copy.wait_send()
    writes[1].wait()
    last_write.wait()


def day_order(days):
    share = days // (NY * NZ * NX)
    place = np.arange(days)
    y, x, t, z = place // (days // NY), (place // (share * NZ)) % NX, (place // NZ) % share, place % NZ
    source = ((y * NZ + z) * NX + x) * share + t
    return jnp.asarray(source[:, None] == place[None, :], jnp.bfloat16)


def main(partials, dest_key, active_from, cohort, decay_rate, peers):
    rows, feats, days = partials.shape
    keys = active_from.shape[0]
    kinds = len(WINDOWS)
    lines = feats * COHORTS
    block_rows = lines // BLOCK * (days // PLANE)
    own_rows = kinds * block_rows // NZ
    padded = -(-own_rows // 8) * 8
    vmem = pl.BlockSpec(memory_space=pltpu.VMEM)
    smem = pl.BlockSpec(memory_space=pltpu.SMEM)
    hbm = pl.BlockSpec(memory_space=pl.ANY)
    half, full = jnp.bfloat16, jnp.float32
    return pl.pallas_call(
        main_kernel,
        out_shape=(
            jax.ShapeDtypeStruct((keys, kinds, feats, days), half),
            jax.ShapeDtypeStruct((kinds, keys), full),
            jax.ShapeDtypeStruct((own_rows, BLOCK), full),
        ),
        in_specs=[smem, hbm, vmem, vmem, vmem, vmem],
        out_specs=(hbm, vmem, vmem),
        scratch_shapes=[
            pltpu.VMEM((rows, feats, days), half),
            pltpu.VMEM((1, peers), jnp.int32),
            pltpu.SMEM((1, peers), jnp.int32),
            pltpu.VMEM((peers, 1, 2 * BLOCK), jnp.int32),
            pltpu.VMEM((DAY_PARTS, peers, feats, BLOCK), half),
            pltpu.VMEM((DAY_PARTS, peers, feats, BLOCK), half),
            pltpu.VMEM((peers, 1, 2 * BLOCK), jnp.int32),
            pltpu.VMEM((peers * feats, BLOCK), full),
            pltpu.VMEM((feats, 2 * BLOCK, kinds * BLOCK), half),
            pltpu.VMEM((feats, keys, BLOCK), half),
            pltpu.VMEM((feats, DAY_PARTS, keys, kinds * BLOCK), half),
            pltpu.VMEM((kinds, keys * feats, BLOCK), full),
            pltpu.VMEM((2, keys, kinds, feats, BLOCK), half),
            pltpu.VMEM((kinds, keys, BLOCK), full),
            pltpu.VMEM((kinds, keys), full),
            pltpu.VMEM((kinds, keys), full),
            pltpu.VMEM((kinds, lines, days), full),
            pltpu.VMEM((PLANE, block_rows, BLOCK), full),
            pltpu.VMEM((kinds, PLANE, block_rows, BLOCK), half),
            pltpu.VMEM((kinds, PLANE, block_rows, BLOCK), half),
            pltpu.VMEM((kinds * block_rows, BLOCK), full),
            pltpu.VMEM((NZ, padded, BLOCK), full),
            pltpu.VMEM((NZ, padded, BLOCK), full),
            pltpu.SemaphoreType.DMA,
            pltpu.SemaphoreType.DMA((DAY_PARTS + 1,)),
            pltpu.SemaphoreType.DMA((DAY_PARTS + 1,)),
            pltpu.SemaphoreType.DMA((2,)),
            pltpu.SemaphoreType.DMA((DAY_PARTS,)),
            pltpu.SemaphoreType.DMA((2, kinds, PLANE)),
            pltpu.SemaphoreType.DMA((2, NZ)),
        ],
        compiler_params=pltpu.CompilerParams(
            collective_id=0, has_side_effects=True, vmem_limit_bytes=60 << 20
        ),
    )(
        decay_rate,
        partials,
        dest_key.reshape(1, rows),
        active_from.reshape(1, keys),
        cohort.reshape(1, keys),
        day_order(days),
    )


def scale_kernel(scale_ref, raw_ref, out_ref):
    block, kinds = raw_ref.shape[:2]
    step = pl.program_id(0)
    for local in range(block):
        for w in range(kinds):
            value = raw_ref[local, w].astype(jnp.float32) * scale_ref[w, step * block + local]
            out_ref[local, w] = value.astype(jnp.bfloat16)


def scale(raw, norm_scale):
    keys, kinds, feats, days = raw.shape
    block = 16
    spec = pl.BlockSpec((block, kinds, feats, days), lambda i: (i, 0, 0, 0))
    return pl.pallas_call(
        scale_kernel,
        grid=(keys // block,),
        out_shape=jax.ShapeDtypeStruct(raw.shape, jnp.bfloat16),
        in_specs=[pl.BlockSpec(memory_space=pltpu.SMEM), spec],
        out_specs=spec,
        compiler_params=pltpu.CompilerParams(vmem_limit_bytes=60 << 20),
    )(norm_scale, raw)


def on_device(partials, dest_key, active_from, cohort, decay_rate):
    key_devs = lax.axis_size("key")
    _, feat_count, day_count = partials.shape
    raw, norm_scale, own = main(partials, dest_key, active_from, cohort, decay_rate, key_devs)
    windowed = scale(raw, norm_scale)
    kinds = len(WINDOWS)
    share = day_count // key_devs
    own = own.reshape(kinds, feat_count * COHORTS // BLOCK, share, BLOCK // COHORTS, COHORTS)
    own = own.transpose(4, 0, 1, 3, 2)
    return (windowed, own.reshape(COHORTS, kinds, feat_count, share))


def solution(mesh):
    placed = (P("key", "feat", None), P("key"), P("key"), P("key"), P(None, "feat"))
    return jax.shard_map(
        on_device,
        mesh=mesh,
        in_specs=placed,
        out_specs=(P("key", None, "feat", None), P(None, None, "feat", "key")),
        check_vma=False,
    )
```

```python
import functools

import jax
import jax.numpy as jnp
import numpy as np
from jax import lax
from jax.experimental import pallas as pl
from jax.experimental.pallas import tpu as pltpu
from jax.sharding import PartitionSpec as P

FEAT = 64
BLOCK = 128
WINDOWS = (7, 28, 91)
COHORTS = 16
NY, NZ, NX = 4, 8, 4
PLANE = NY * NX
MESH = pl.DeviceIdType.MESH


DAY_PARTS = 3
PARTS = ((0, 0, 1), (1, 0, 1), (2, 0, 2), (2, 1, 2))
AT_ONCE = 8


def peer_at(me, step):
    y, z, x = me // (NZ * NX), (me // NX) % NZ, me % NX
    dy, dz, dx = step // (NZ * NX), (step // NX) % NZ, step % NX
    return ((y + dy) % NY) * (NZ * NX) + ((z + dz) % NZ) * NX + (x + dx) % NX


def far_first(peers):
    def distance(step):
        place = (step // (NZ * NX), NY), ((step // NX) % NZ, NZ), (step % NX, NX)
        return sum(min(d, n - d) for d, n in place)

    return sorted(range(1, peers), key=lambda step: (-distance(step), step))


def send_to(source, target, send_sem, recv_sem, where):
    copy = pltpu.make_async_remote_copy(
        src_ref=source,
        dst_ref=target,
        send_sem=send_sem,
        recv_sem=recv_sem,
        device_id=where,
        device_id_type=MESH,
    )
    copy.start()
    return copy


def main_kernel(
    rate_ref,
    rows_ref,
    dest_ref,
    start_ref,
    cohort_ref,
    order_ref,
    raw_ref,
    norm_ref,
    mean_ref,
    held,
    slot_row,
    slot_ref,
    note_ref,
    packed,
    landed,
    note_landed,
    wide,
    bands,
    before,
    kept,
    spread,
    staged,
    squares,
    share_out,
    share_in,
    table,
    turned,
    block_out,
    block_in,
    sums,
    piece_out,
    piece_in,
    load_sem,
    send_sems,
    recv_sems,
    pair_sems,
    out_sems,
    block_sems,
    piece_sems,
):
    me = lax.axis_index("key")
    other = {"feat": 1 - lax.axis_index("feat")}
    y, z, x = me // (NZ * NX), (me // NX) % NZ, me % NX
    peers, feats, _ = landed[0].shape
    keys = start_ref.shape[1]
    kinds = len(WINDOWS)
    load = pltpu.make_async_copy(rows_ref, held, load_sem)
    load.start()
    barrier = pltpu.get_barrier_semaphore()

    for step in far_first(peers):
        pl.semaphore_signal(barrier, 1, device_id={"key": peer_at(me, step)}, device_id_type=MESH)
    pl.semaphore_signal(barrier, 1, device_id=other, device_id_type=MESH)

    row_count = held.shape[0]
    square = (peers, BLOCK)
    sub = lax.broadcasted_iota(jnp.int32, square, 0)
    lane = lax.broadcasted_iota(jnp.int32, square, 1)

    def down(row):
        return jnp.broadcast_to(row, square).T

    dest = jnp.broadcast_to(dest_ref[...], (peers, row_count)).T
    match = dest // keys == lane[:row_count]
    slot_row[...] = jnp.max(jnp.where(match, sub[:row_count], 0), axis=0, keepdims=True)
    to_scalar = pltpu.make_async_copy(slot_row, slot_ref, pair_sems.at[0])
    to_scalar.start()
    slot_key = jnp.max(jnp.where(match, dest % keys, -1), axis=0, keepdims=True)
    note_ref[:, 0, :BLOCK] = down(slot_key)
    in_cohort = down(cohort_ref[...]) == lane % COHORTS
    part_count = jnp.sum(jnp.where(in_cohort, 1, 0), axis=0, keepdims=True)
    note_ref[:, 0, BLOCK:] = jnp.broadcast_to(part_count, square)
    to_scalar.wait()
    load.wait()
    pl.semaphore_wait(barrier, peers)

    notes_at = len(PARTS)
    for part, (day, piece, pieces) in enumerate(PARTS):
        some = slice(piece * feats // pieces, (piece + 1) * feats // pieces)
        days = slice(day * BLOCK, (day + 1) * BLOCK)

        def send(step, carry):
            peer = peer_at(me, step)
            packed[part][step] = held[slot_ref[0, peer], some, days]
            where = {"key": peer}
            send_to(packed[part].at[step], landed[part].at[me], send_sems.at[part], recv_sems.at[part], where)
            if part == 0:
                send_to(note_ref.at[peer], note_landed.at[me], send_sems.at[notes_at], recv_sems.at[notes_at], where)
            return carry

        lax.fori_loop(1, peers, send, 0)
        landed[part][me] = held[slot_ref[0, me], some, days]
    note_landed[me] = note_ref[me]

    shape = (2 * BLOCK, BLOCK)
    lag = BLOCK + lax.broadcasted_iota(jnp.int32, shape, 1) - lax.broadcasted_iota(jnp.int32, shape, 0)
    lag_float = lag.astype(jnp.float32)

    def make_band(f, carry):
        for w, length in enumerate(WINDOWS):
            weights = jnp.exp(-rate_ref[w, f] * lag_float)
            inside = (lag >= 0) & (lag < length)
            band = jnp.where(inside, weights, 0.0).astype(jnp.bfloat16)
            bands[f, :, w * BLOCK : (w + 1) * BLOCK] = band
        return carry

    lax.fori_loop(0, feats, make_band, 0)

    start = down(start_ref[...])
    squares[...] = jnp.zeros_like(squares)

    def whole(source, target, index):
        others = pl.ds(0, peers - 1)
        return pltpu.make_async_remote_copy(
            src_ref=source.at[others],
            dst_ref=target.at[others],
            send_sem=send_sems.at[index],
            recv_sem=recv_sems.at[index],
            device_id={"key": peer_at(me, 1)},
            device_id_type=MESH,
        )

    notes = whole(note_ref, note_landed, notes_at)
    notes.wait_recv()
    arrived = note_landed[:, 0, :BLOCK]
    receive = jnp.where(arrived == lane, 1.0, 0.0).T.astype(jnp.bfloat16)
    count = jnp.sum(note_landed[:, 0, BLOCK:], axis=0, keepdims=True).astype(jnp.float32)

    def pack(part):
        def interleave(f, carry):
            for w in range(kinds):
                piece = kept[f, part, :, w * BLOCK : (w + 1) * BLOCK].astype(jnp.float32)
                spread[w, pl.ds(f, keys, stride=feats), :] = piece
            return carry

        lax.fori_loop(0, feats, interleave, 0, unroll=2)

        def some_keys(some, carry):
            for w in range(kinds):
                spot = pl.ds(pl.multiple_of(some * 4 * feats, 4 * feats), 4 * feats)
                piece = spread[w, spot, :].astype(jnp.bfloat16)
                staged[part % 2, pl.ds(some * 4, 4), w] = piece.reshape(4, feats, BLOCK)
            return carry

        lax.fori_loop(0, keys // 4, some_keys, 0)
        copy = pltpu.make_async_copy(
            staged.at[part % 2],
            raw_ref.at[:, :, :, pl.ds(part * BLOCK, BLOCK)],
            out_sems.at[part],
        )
        copy.start()
        return copy

    writes = []
    for part, (day, piece, pieces) in enumerate(PARTS):
        arrival = whole(packed[part], landed[part], part)
        count_here = feats // pieces
        first = piece * count_here
        arrival.wait_recv()

        def widen(some, carry):
            spot = pl.ds(pl.multiple_of(some * 8 * count_here, 8 * count_here), 8 * count_here)
            piece = landed[part][pl.ds(some * 8, 8)].astype(jnp.float32)
            wide[spot, :] = piece.reshape(8 * count_here, BLOCK)
            return carry

        lax.fori_loop(0, peers // 8, widen, 0)
        live = lane + day * BLOCK >= start

        def features(group, carry):
            columns = []
            for local in range(AT_ONCE):
                f = group * AT_ONCE + local
                columns.append(wide[pl.ds(f, peers, stride=count_here), :].astype(jnp.bfloat16))
            summed = jnp.dot(receive, jnp.concatenate(columns, axis=1), preferred_element_type=jnp.float32)
            results = []
            for local in range(AT_ONCE):
                f = first + group * AT_ONCE + local
                daily = summed[:, local * BLOCK : (local + 1) * BLOCK]
                daily = jnp.where(live, daily, 0.0).astype(jnp.bfloat16)
                if day == 0:
                    result = jnp.dot(daily, bands[f, BLOCK:, :], preferred_element_type=jnp.float32)
                else:
                    both = jnp.concatenate([before[f], daily], axis=1)
                    result = jnp.dot(both, bands[f], preferred_element_type=jnp.float32)
                if day < DAY_PARTS - 1:
                    before[f] = daily
                kept[f, day] = result.astype(jnp.bfloat16)
                results.append(result)
            for w in range(kinds):
                pieces = [result[:, w * BLOCK : (w + 1) * BLOCK] for result in results]
                squares[w] += sum(piece * piece for piece in pieces)
            return carry

        lax.fori_loop(0, count_here // AT_ONCE, features, 0)
        if day < DAY_PARTS - 1:
            writes.append(pack(day))

    for w in range(kinds):
        share_out[w : w + 1, :] = jnp.sum(squares[w].T, axis=0, keepdims=True)
    share = send_to(share_out, share_in, pair_sems.at[0], pair_sems.at[1], other)
    share.wait()
    mean_square = (share_out[...] + share_in[...]) / (FEAT * DAY_PARTS * BLOCK)
    norm = lax.rsqrt(mean_square + 1e-05)
    norm_ref[...] = norm
    cohort_row = lax.broadcasted_iota(jnp.int32, (COHORTS, keys), 0)
    member = cohort_row == jnp.broadcast_to(cohort_ref[...], (COHORTS, keys))
    weights = []
    for w in range(kinds):
        scaled = jnp.where(member, norm[w : w + 1, :], 0.0)
        high = scaled.astype(jnp.bfloat16)
        low = (scaled - high.astype(jnp.float32)).astype(jnp.bfloat16)
        weights.append(jnp.concatenate([high, low], axis=0))

    def plane_peer(step):
        ty, tx = (y + step // NX) % NY, (x + step % NX) % NX
        return (ty * NZ + z) * NX + tx, ty * NX + tx

    def line_peer(step):
        tz = (z + step) % NZ
        return (y * NZ + tz) * NX + x, tz

    rows = block_out.shape[2]
    each = order_ref.shape[0] // PLANE
    block_copies = []
    for w in range(kinds):
        lanes = slice(w * BLOCK, (w + 1) * BLOCK)

        def add_cohorts(group, carry):
            for local in range(AT_ONCE):
                f = group * AT_ONCE + local
                spot = pl.ds(pl.multiple_of(f * COHORTS, COHORTS), COHORTS)
                for day in range(DAY_PARTS):
                    result = jnp.dot(weights[w], kept[f, day, :, lanes], preferred_element_type=jnp.float32)
                    both = result[:COHORTS] + result[COHORTS:]
                    table[w, spot, day * BLOCK : (day + 1) * BLOCK] = both
            return carry

        lax.fori_loop(0, feats // AT_ONCE, add_cohorts, 0)
        for g in range(rows // each):
            lines = table[w, g * BLOCK : (g + 1) * BLOCK, :].astype(jnp.bfloat16)
            by_day = lax.dot_general(
                order_ref[...], lines, (((1,), (1,)), ((), ())), preferred_element_type=jnp.float32
            )
            turned[:, g * each : (g + 1) * each, :] = by_day.reshape(PLANE, each, BLOCK)
        block_out[w] = turned[...].astype(jnp.bfloat16)
        for step in range(1, PLANE):
            peer, block = plane_peer(step)
            sems = block_sems.at[0, w, step], block_sems.at[1, w, step]
            block_copies.append(
                send_to(block_out.at[w, block], block_in.at[w, step], *sems, {"key": peer})
            )
    writes[0].wait()
    last_write = pack(DAY_PARTS - 1)
    for w in range(kinds):
        total = block_out[w, y * NX + x].astype(jnp.float32)
        for step in range(1, PLANE):
            block_copies[w * (PLANE - 1) + step - 1].wait_recv()
            total = total + block_in[w, step].astype(jnp.float32)
        sums[w * rows : (w + 1) * rows, :] = total
    own_rows, held_rows = mean_ref.shape[0], piece_out.shape[1]
    filled = kinds * rows
    sums[filled:, :] = jnp.zeros((held_rows * NZ - filled, BLOCK), jnp.float32)
    for tz in range(NZ):
        piece_out[tz] = sums[pl.ds(tz, held_rows, stride=NZ), :].astype(jnp.bfloat16)
    piece_copies = []
    for step in range(1, NZ):
        peer, block = line_peer(step)
        sems = piece_sems.at[0, step], piece_sems.at[1, step]
        piece_copies.append(send_to(piece_out.at[block], piece_in.at[step], *sems, {"key": peer}))
    total = piece_out[z].astype(jnp.float32)
    for step in range(1, NZ):
        piece_copies[step - 1].wait_recv()
        total = total + piece_in[step].astype(jnp.float32)
    mean_ref[...] = total[:own_rows] / jnp.maximum(count, 1.0)

    for part in range(len(PARTS)):
        whole(packed[part], landed[part], part).wait_send()
    notes.wait_send()
    for copy in block_copies + piece_copies:
        copy.wait_send()
    writes[1].wait()
    last_write.wait()


def day_order(days):
    share = days // (NY * NZ * NX)
    place = np.arange(days)
    y, x, t, z = place // (days // NY), (place // (share * NZ)) % NX, (place // NZ) % share, place % NZ
    source = ((y * NZ + z) * NX + x) * share + t
    return jnp.asarray(source[:, None] == place[None, :], jnp.bfloat16)


def main(partials, dest_key, active_from, cohort, decay_rate, peers):
    rows, feats, days = partials.shape
    keys = active_from.shape[0]
    kinds = len(WINDOWS)
    lines = feats * COHORTS
    block_rows = lines // BLOCK * (days // PLANE)
    own_rows = kinds * block_rows // NZ
    padded = -(-own_rows // 16) * 16
    vmem = pl.BlockSpec(memory_space=pltpu.VMEM)
    smem = pl.BlockSpec(memory_space=pltpu.SMEM)
    hbm = pl.BlockSpec(memory_space=pl.ANY)
    half, full = jnp.bfloat16, jnp.float32
    return pl.pallas_call(
        main_kernel,
        out_shape=(
            jax.ShapeDtypeStruct((keys, kinds, feats, days), half),
            jax.ShapeDtypeStruct((kinds, keys), full),
            jax.ShapeDtypeStruct((own_rows, BLOCK), full),
        ),
        in_specs=[smem, hbm, vmem, vmem, vmem, vmem],
        out_specs=(hbm, vmem, vmem),
        scratch_shapes=[
            pltpu.VMEM((rows, feats, days), half),
            pltpu.VMEM((1, peers), jnp.int32),
            pltpu.SMEM((1, peers), jnp.int32),
            pltpu.VMEM((peers, 1, 2 * BLOCK), jnp.int32),
            [pltpu.VMEM((peers, feats // n, BLOCK), half) for _, _, n in PARTS],
            [pltpu.VMEM((peers, feats // n, BLOCK), half) for _, _, n in PARTS],
            pltpu.VMEM((peers, 1, 2 * BLOCK), jnp.int32),
            pltpu.VMEM((peers * feats, BLOCK), full),
            pltpu.VMEM((feats, 2 * BLOCK, kinds * BLOCK), half),
            pltpu.VMEM((feats, keys, BLOCK), half),
            pltpu.VMEM((feats, DAY_PARTS, keys, kinds * BLOCK), half),
            pltpu.VMEM((kinds, keys * feats, BLOCK), full),
            pltpu.VMEM((2, keys, kinds, feats, BLOCK), half),
            pltpu.VMEM((kinds, keys, BLOCK), full),
            pltpu.VMEM((kinds, keys), full),
            pltpu.VMEM((kinds, keys), full),
            pltpu.VMEM((kinds, lines, days), full),
            pltpu.VMEM((PLANE, block_rows, BLOCK), full),
            pltpu.VMEM((kinds, PLANE, block_rows, BLOCK), half),
            pltpu.VMEM((kinds, PLANE, block_rows, BLOCK), half),
            pltpu.VMEM((padded * NZ, BLOCK), full),
            pltpu.VMEM((NZ, padded, BLOCK), half),
            pltpu.VMEM((NZ, padded, BLOCK), half),
            pltpu.SemaphoreType.DMA,
            pltpu.SemaphoreType.DMA((len(PARTS) + 1,)),
            pltpu.SemaphoreType.DMA((len(PARTS) + 1,)),
            pltpu.SemaphoreType.DMA((2,)),
            pltpu.SemaphoreType.DMA((DAY_PARTS,)),
            pltpu.SemaphoreType.DMA((2, kinds, PLANE)),
            pltpu.SemaphoreType.DMA((2, NZ)),
        ],
        compiler_params=pltpu.CompilerParams(
            collective_id=0, has_side_effects=True, vmem_limit_bytes=60 << 20
        ),
    )(
        decay_rate,
        partials,
        dest_key.reshape(1, rows),
        active_from.reshape(1, keys),
        cohort.reshape(1, keys),
        day_order(days),
    )


def scale_kernel(scale_ref, raw_ref, out_ref, taken, given, in_sems, out_sems):
    keys, kinds = taken.shape[:2]
    parts = in_sems.shape[0]
    block = keys // parts

    def spot(part):
        return pl.ds(part * block, block)

    def read(part):
        return pltpu.make_async_copy(raw_ref.at[spot(part)], taken.at[spot(part)], in_sems.at[part])

    def write(part):
        return pltpu.make_async_copy(given.at[spot(part)], out_ref.at[spot(part)], out_sems.at[part])

    for part in range(parts):
        read(part).start()
    for part in range(parts):
        read(part).wait()

        def pair(index, carry):
            for local in range(2):
                key = part * block + index * 2 + local
                for w in range(kinds):
                    value = taken[key, w].astype(jnp.float32) * scale_ref[w, key]
                    given[key, w] = value.astype(jnp.bfloat16)
            return carry

        lax.fori_loop(0, block // 2, pair, 0)
        write(part).start()
    for part in range(parts):
        write(part).wait()


def scale(raw, norm_scale):
    hbm = pl.BlockSpec(memory_space=pl.ANY)
    parts = 8
    return pl.pallas_call(
        scale_kernel,
        out_shape=jax.ShapeDtypeStruct(raw.shape, jnp.bfloat16),
        in_specs=[pl.BlockSpec(memory_space=pltpu.SMEM), hbm],
        out_specs=hbm,
        scratch_shapes=[
            pltpu.VMEM(raw.shape, jnp.bfloat16),
            pltpu.VMEM(raw.shape, jnp.bfloat16),
            pltpu.SemaphoreType.DMA((parts,)),
            pltpu.SemaphoreType.DMA((parts,)),
        ],
        compiler_params=pltpu.CompilerParams(vmem_limit_bytes=60 << 20),
    )(norm_scale, raw)


def on_device(partials, dest_key, active_from, cohort, decay_rate):
    key_devs = lax.axis_size("key")
    _, feat_count, day_count = partials.shape
    raw, norm_scale, own = main(partials, dest_key, active_from, cohort, decay_rate, key_devs)
    windowed = scale(raw, norm_scale)
    kinds = len(WINDOWS)
    share = day_count // key_devs
    own = own.reshape(kinds, feat_count * COHORTS // BLOCK, share, BLOCK // COHORTS, COHORTS)
    own = own.transpose(4, 0, 1, 3, 2)
    return (windowed, own.reshape(COHORTS, kinds, feat_count, share))


def solution(mesh):
    placed = (P("key", "feat", None), P("key"), P("key"), P("key"), P(None, "feat"))
    return jax.shard_map(
        on_device,
        mesh=mesh,
        in_specs=placed,
        out_specs=(P("key", None, "feat", None), P(None, None, "feat", "key")),
        check_vma=False,
    )
```

```python
import functools

import jax
import jax.numpy as jnp
import numpy as np
from jax import lax
from jax.experimental import pallas as pl
from jax.experimental.pallas import tpu as pltpu
from jax.sharding import PartitionSpec as P

FEAT = 64
BLOCK = 128
WINDOWS = (7, 28, 91)
COHORTS = 16
NY, NZ, NX = 4, 8, 4
PLANE = NY * NX
MESH = pl.DeviceIdType.MESH


DAY_PARTS = 3
PARTS = ((0, 0, 1), (1, 0, 1), (2, 0, 2), (2, 1, 2))
AT_ONCE = 8


def peer_at(me, step):
    y, z, x = me // (NZ * NX), (me // NX) % NZ, me % NX
    dy, dz, dx = step // (NZ * NX), (step // NX) % NZ, step % NX
    return ((y + dy) % NY) * (NZ * NX) + ((z + dz) % NZ) * NX + (x + dx) % NX


def far_first(peers):
    def distance(step):
        place = (step // (NZ * NX), NY), ((step // NX) % NZ, NZ), (step % NX, NX)
        return sum(min(d, n - d) for d, n in place)

    return sorted(range(1, peers), key=lambda step: (-distance(step), step))


def send_to(source, target, send_sem, recv_sem, where):
    copy = pltpu.make_async_remote_copy(
        src_ref=source,
        dst_ref=target,
        send_sem=send_sem,
        recv_sem=recv_sem,
        device_id=where,
        device_id_type=MESH,
    )
    copy.start()
    return copy


def main_kernel(
    rate_ref,
    rows_ref,
    dest_ref,
    start_ref,
    cohort_ref,
    order_ref,
    raw_ref,
    norm_ref,
    mean_ref,
    held,
    slot_row,
    slot_ref,
    note_ref,
    packed,
    landed,
    note_landed,
    wide,
    bands,
    before,
    kept,
    spread,
    staged,
    squares,
    share_out,
    share_in,
    table,
    turned,
    block_out,
    first_in,
    middle,
    second_in,
    sums,
    piece_out,
    piece_in,
    load_sem,
    send_sems,
    recv_sems,
    pair_sems,
    out_sems,
    block_sems,
    piece_sems,
):
    me = lax.axis_index("key")
    other = {"feat": 1 - lax.axis_index("feat")}
    y, z, x = me // (NZ * NX), (me // NX) % NZ, me % NX
    peers, feats, _ = landed[0].shape
    keys = start_ref.shape[1]
    kinds = len(WINDOWS)
    load = pltpu.make_async_copy(rows_ref, held, load_sem)
    load.start()
    barrier = pltpu.get_barrier_semaphore()

    for step in far_first(peers):
        pl.semaphore_signal(barrier, 1, device_id={"key": peer_at(me, step)}, device_id_type=MESH)
    pl.semaphore_signal(barrier, 1, device_id=other, device_id_type=MESH)

    row_count = held.shape[0]
    square = (peers, BLOCK)
    sub = lax.broadcasted_iota(jnp.int32, square, 0)
    lane = lax.broadcasted_iota(jnp.int32, square, 1)

    def down(row):
        return jnp.broadcast_to(row, square).T

    dest = jnp.broadcast_to(dest_ref[...], (peers, row_count)).T
    match = dest // keys == lane[:row_count]
    slot_row[...] = jnp.max(jnp.where(match, sub[:row_count], 0), axis=0, keepdims=True)
    to_scalar = pltpu.make_async_copy(slot_row, slot_ref, pair_sems.at[0])
    to_scalar.start()
    slot_key = jnp.max(jnp.where(match, dest % keys, -1), axis=0, keepdims=True)
    note_ref[:, 0, :BLOCK] = down(slot_key)
    in_cohort = down(cohort_ref[...]) == lane % COHORTS
    part_count = jnp.sum(jnp.where(in_cohort, 1, 0), axis=0, keepdims=True)
    note_ref[:, 0, BLOCK:] = jnp.broadcast_to(part_count, square)
    to_scalar.wait()
    load.wait()
    pl.semaphore_wait(barrier, peers)

    notes_at = len(PARTS)
    for part, (day, piece, pieces) in enumerate(PARTS):
        some = slice(piece * feats // pieces, (piece + 1) * feats // pieces)
        days = slice(day * BLOCK, (day + 1) * BLOCK)

        def send(step, carry):
            peer = peer_at(me, step)
            packed[part][step] = held[slot_ref[0, peer], some, days]
            where = {"key": peer}
            send_to(packed[part].at[step], landed[part].at[me], send_sems.at[part], recv_sems.at[part], where)
            if part == 0:
                send_to(note_ref.at[peer], note_landed.at[me], send_sems.at[notes_at], recv_sems.at[notes_at], where)
            return carry

        lax.fori_loop(1, peers, send, 0)
        landed[part][me] = held[slot_ref[0, me], some, days]
    note_landed[me] = note_ref[me]

    shape = (2 * BLOCK, BLOCK)
    lag = BLOCK + lax.broadcasted_iota(jnp.int32, shape, 1) - lax.broadcasted_iota(jnp.int32, shape, 0)
    lag_float = lag.astype(jnp.float32)

    def make_band(f, carry):
        for w, length in enumerate(WINDOWS):
            weights = jnp.exp(-rate_ref[w, f] * lag_float)
            inside = (lag >= 0) & (lag < length)
            band = jnp.where(inside, weights, 0.0).astype(jnp.bfloat16)
            bands[f, :, w * BLOCK : (w + 1) * BLOCK] = band
        return carry

    lax.fori_loop(0, feats, make_band, 0)

    start = down(start_ref[...])
    squares[...] = jnp.zeros_like(squares)

    def whole(source, target, index):
        others = pl.ds(0, peers - 1)
        return pltpu.make_async_remote_copy(
            src_ref=source.at[others],
            dst_ref=target.at[others],
            send_sem=send_sems.at[index],
            recv_sem=recv_sems.at[index],
            device_id={"key": peer_at(me, 1)},
            device_id_type=MESH,
        )

    notes = whole(note_ref, note_landed, notes_at)
    notes.wait_recv()
    arrived = note_landed[:, 0, :BLOCK]
    receive = jnp.where(arrived == lane, 1.0, 0.0).T.astype(jnp.bfloat16)
    count = jnp.sum(note_landed[:, 0, BLOCK:], axis=0, keepdims=True).astype(jnp.float32)

    def interleave_day(part):
        def interleave(f, carry):
            for w in range(kinds):
                piece = kept[f, part, :, w * BLOCK : (w + 1) * BLOCK].astype(jnp.float32)
                spread[w, pl.ds(f, keys, stride=feats), :] = piece
            return carry

        lax.fori_loop(0, feats, interleave, 0, unroll=2)

    def pack(part):
        def some_keys(some, carry):
            for w in range(kinds):
                spot = pl.ds(pl.multiple_of(some * 4 * feats, 4 * feats), 4 * feats)
                piece = spread[w, spot, :].astype(jnp.bfloat16)
                staged[part % 2, pl.ds(some * 4, 4), w] = piece.reshape(4, feats, BLOCK)
            return carry

        lax.fori_loop(0, keys // 4, some_keys, 0)
        copy = pltpu.make_async_copy(
            staged.at[part % 2],
            raw_ref.at[:, :, :, pl.ds(part * BLOCK, BLOCK)],
            out_sems.at[part],
        )
        copy.start()
        return copy

    writes = []
    for part, (day, piece, pieces) in enumerate(PARTS):
        arrival = whole(packed[part], landed[part], part)
        count_here = feats // pieces
        first = piece * count_here
        arrival.wait_recv()

        def widen(some, carry):
            spot = pl.ds(pl.multiple_of(some * 8 * count_here, 8 * count_here), 8 * count_here)
            piece = landed[part][pl.ds(some * 8, 8)].astype(jnp.float32)
            wide[spot, :] = piece.reshape(8 * count_here, BLOCK)
            return carry

        lax.fori_loop(0, peers // 8, widen, 0)
        live = lane + day * BLOCK >= start

        def features(group, carry):
            columns = []
            for local in range(AT_ONCE):
                f = group * AT_ONCE + local
                columns.append(wide[pl.ds(f, peers, stride=count_here), :].astype(jnp.bfloat16))
            summed = jnp.dot(receive, jnp.concatenate(columns, axis=1), preferred_element_type=jnp.float32)
            results = []
            for local in range(AT_ONCE):
                f = first + group * AT_ONCE + local
                daily = summed[:, local * BLOCK : (local + 1) * BLOCK]
                daily = jnp.where(live, daily, 0.0).astype(jnp.bfloat16)
                if day == 0:
                    result = jnp.dot(daily, bands[f, BLOCK:, :], preferred_element_type=jnp.float32)
                else:
                    both = jnp.concatenate([before[f], daily], axis=1)
                    result = jnp.dot(both, bands[f], preferred_element_type=jnp.float32)
                if day < DAY_PARTS - 1:
                    before[f] = daily
                kept[f, day] = result.astype(jnp.bfloat16)
                results.append(result)
            for w in range(kinds):
                pieces = [result[:, w * BLOCK : (w + 1) * BLOCK] for result in results]
                squares[w] += sum(piece * piece for piece in pieces)
            return carry

        lax.fori_loop(0, count_here // AT_ONCE, features, 0)
        if day < DAY_PARTS - 1:
            interleave_day(day)
            writes.append(pack(day))

    for w in range(kinds):
        share_out[w : w + 1, :] = jnp.sum(squares[w].T, axis=0, keepdims=True)
    share = send_to(share_out, share_in, pair_sems.at[0], pair_sems.at[1], other)
    share.wait()
    mean_square = (share_out[...] + share_in[...]) / (FEAT * DAY_PARTS * BLOCK)
    norm = lax.rsqrt(mean_square + 1e-05)
    norm_ref[...] = norm
    cohort_row = lax.broadcasted_iota(jnp.int32, (COHORTS, keys), 0)
    member = cohort_row == jnp.broadcast_to(cohort_ref[...], (COHORTS, keys))
    weights = []
    for w in range(kinds):
        scaled = jnp.where(member, norm[w : w + 1, :], 0.0)
        high = scaled.astype(jnp.bfloat16)
        low = (scaled - high.astype(jnp.float32)).astype(jnp.bfloat16)
        weights.append(jnp.concatenate([high, low], axis=0))

    def column_peer(step):
        ty = (y + step) % NY
        return (ty * NZ + z) * NX + x, ty

    def row_peer(step):
        tx = (x + step) % NX
        return (y * NZ + z) * NX + tx, tx

    def line_peer(step):
        tz = (z + step) % NZ
        return (y * NZ + tz) * NX + x, tz

    rows = block_out.shape[3]
    half = rows // 2
    upper, lower = pl.ds(0, half), pl.ds(half, half)
    each = order_ref.shape[0] // PLANE
    first_copies, second_copies = [], []
    for w in range(kinds):
        lanes = slice(w * BLOCK, (w + 1) * BLOCK)

        def add_cohorts(group, carry):
            for local in range(AT_ONCE):
                f = group * AT_ONCE + local
                spot = pl.ds(pl.multiple_of(f * COHORTS, COHORTS), COHORTS)
                for day in range(DAY_PARTS):
                    result = jnp.dot(weights[w], kept[f, day, :, lanes], preferred_element_type=jnp.float32)
                    both = result[:COHORTS] + result[COHORTS:]
                    table[w, spot, day * BLOCK : (day + 1) * BLOCK] = both
            return carry

        lax.fori_loop(0, feats // AT_ONCE, add_cohorts, 0)
        for g in range(rows // each):
            lines = table[w, g * BLOCK : (g + 1) * BLOCK, :].astype(jnp.bfloat16)
            by_day = lax.dot_general(
                order_ref[...], lines, (((1,), (1,)), ((), ())), preferred_element_type=jnp.float32
            )
            turned[:, g * each : (g + 1) * each, :] = by_day.reshape(PLANE, each, BLOCK)
        block_out[w] = turned[...].astype(jnp.bfloat16).reshape(block_out.shape[1:])
        for step in range(1, NX):
            peer, place = row_peer(step)
            sems = block_sems.at[0, w, 0, step], block_sems.at[1, w, 0, step]
            source = block_out.at[w, :, place, upper]
            first_copies.append(send_to(source, first_in.at[w, 0, step], *sems, {"key": peer}))
            peer, place = column_peer(step)
            sems = block_sems.at[0, w, 1, step], block_sems.at[1, w, 1, step]
            source = block_out.at[w, place, :, lower]
            first_copies.append(send_to(source, first_in.at[w, 1, step], *sems, {"key": peer}))
    interleave_day(DAY_PARTS - 1)
    for w in range(kinds):
        for copy in first_copies[w * 2 * (NX - 1) : (w + 1) * 2 * (NX - 1)]:
            copy.wait_recv()
        for side in range(2):
            own = block_out[w, :, x, :half] if side == 0 else block_out[w, y, :, half:]
            total = own.astype(jnp.float32)
            for step in range(1, NX):
                total = total + first_in[w, side, step].astype(jnp.float32)
            middle[w, side] = total.astype(jnp.bfloat16)
        for step in range(1, NX):
            peer, place = column_peer(step)
            sems = block_sems.at[0, w, 2, step], block_sems.at[1, w, 2, step]
            source = middle.at[w, 0, place]
            second_copies.append(send_to(source, second_in.at[w, 0, step], *sems, {"key": peer}))
            peer, place = row_peer(step)
            sems = block_sems.at[0, w, 3, step], block_sems.at[1, w, 3, step]
            source = middle.at[w, 1, place]
            second_copies.append(send_to(source, second_in.at[w, 1, step], *sems, {"key": peer}))
    writes[0].wait()
    last_write = pack(DAY_PARTS - 1)
    for w in range(kinds):
        for copy in second_copies[w * 2 * (NX - 1) : (w + 1) * 2 * (NX - 1)]:
            copy.wait_recv()
        for side, place in ((0, y), (1, x)):
            total = middle[w, side, place].astype(jnp.float32)
            for step in range(1, NX):
                total = total + second_in[w, side, step].astype(jnp.float32)
            sums[w * rows + side * half : w * rows + (side + 1) * half, :] = total
    own_rows, held_rows = mean_ref.shape[0], piece_out.shape[1]
    filled = kinds * rows
    sums[filled:, :] = jnp.zeros((held_rows * NZ - filled, BLOCK), jnp.float32)
    for tz in range(NZ):
        piece_out[tz] = sums[pl.ds(tz, held_rows, stride=NZ), :].astype(jnp.bfloat16)
    piece_copies = []
    for step in range(1, NZ):
        peer, block = line_peer(step)
        sems = piece_sems.at[0, step], piece_sems.at[1, step]
        piece_copies.append(send_to(piece_out.at[block], piece_in.at[step], *sems, {"key": peer}))
    total = piece_out[z].astype(jnp.float32)
    for step in range(1, NZ):
        piece_copies[step - 1].wait_recv()
        total = total + piece_in[step].astype(jnp.float32)
    mean_ref[...] = total[:own_rows] / jnp.maximum(count, 1.0)

    for part in range(len(PARTS)):
        whole(packed[part], landed[part], part).wait_send()
    notes.wait_send()
    for copy in first_copies + second_copies + piece_copies:
        copy.wait_send()
    writes[1].wait()
    last_write.wait()


def day_order(days):
    share = days // (NY * NZ * NX)
    place = np.arange(days)
    y, x, t, z = place // (days // NY), (place // (share * NZ)) % NX, (place // NZ) % share, place % NZ
    source = ((y * NZ + z) * NX + x) * share + t
    return jnp.asarray(source[:, None] == place[None, :], jnp.bfloat16)


def main(partials, dest_key, active_from, cohort, decay_rate, peers):
    rows, feats, days = partials.shape
    keys = active_from.shape[0]
    kinds = len(WINDOWS)
    lines = feats * COHORTS
    block_rows = lines // BLOCK * (days // PLANE)
    own_rows = kinds * block_rows // NZ
    padded = -(-own_rows // 16) * 16
    vmem = pl.BlockSpec(memory_space=pltpu.VMEM)
    smem = pl.BlockSpec(memory_space=pltpu.SMEM)
    hbm = pl.BlockSpec(memory_space=pl.ANY)
    half, full = jnp.bfloat16, jnp.float32
    return pl.pallas_call(
        main_kernel,
        out_shape=(
            jax.ShapeDtypeStruct((keys, kinds, feats, days), half),
            jax.ShapeDtypeStruct((kinds, keys), full),
            jax.ShapeDtypeStruct((own_rows, BLOCK), full),
        ),
        in_specs=[smem, hbm, vmem, vmem, vmem, vmem],
        out_specs=(hbm, vmem, vmem),
        scratch_shapes=[
            pltpu.VMEM((rows, feats, days), half),
            pltpu.VMEM((1, peers), jnp.int32),
            pltpu.SMEM((1, peers), jnp.int32),
            pltpu.VMEM((peers, 1, 2 * BLOCK), jnp.int32),
            [pltpu.VMEM((peers, feats // n, BLOCK), half) for _, _, n in PARTS],
            [pltpu.VMEM((peers, feats // n, BLOCK), half) for _, _, n in PARTS],
            pltpu.VMEM((peers, 1, 2 * BLOCK), jnp.int32),
            pltpu.VMEM((peers * feats, BLOCK), full),
            pltpu.VMEM((feats, 2 * BLOCK, kinds * BLOCK), half),
            pltpu.VMEM((feats, keys, BLOCK), half),
            pltpu.VMEM((feats, DAY_PARTS, keys, kinds * BLOCK), half),
            pltpu.VMEM((kinds, keys * feats, BLOCK), full),
            pltpu.VMEM((2, keys, kinds, feats, BLOCK), half),
            pltpu.VMEM((kinds, keys, BLOCK), full),
            pltpu.VMEM((kinds, keys), full),
            pltpu.VMEM((kinds, keys), full),
            pltpu.VMEM((kinds, lines, days), full),
            pltpu.VMEM((PLANE, block_rows, BLOCK), full),
            pltpu.VMEM((kinds, NY, NX, block_rows, BLOCK), half),
            pltpu.VMEM((kinds, 2, NX, NY, block_rows // 2, BLOCK), half),
            pltpu.VMEM((kinds, 2, NY, block_rows // 2, BLOCK), half),
            pltpu.VMEM((kinds, 2, NX, block_rows // 2, BLOCK), half),
            pltpu.VMEM((padded * NZ, BLOCK), full),
            pltpu.VMEM((NZ, padded, BLOCK), half),
            pltpu.VMEM((NZ, padded, BLOCK), half),
            pltpu.SemaphoreType.DMA,
            pltpu.SemaphoreType.DMA((len(PARTS) + 1,)),
            pltpu.SemaphoreType.DMA((len(PARTS) + 1,)),
            pltpu.SemaphoreType.DMA((2,)),
            pltpu.SemaphoreType.DMA((DAY_PARTS,)),
            pltpu.SemaphoreType.DMA((2, kinds, 4, NX)),
            pltpu.SemaphoreType.DMA((2, NZ)),
        ],
        compiler_params=pltpu.CompilerParams(
            collective_id=0, has_side_effects=True, vmem_limit_bytes=60 << 20
        ),
    )(
        decay_rate,
        partials,
        dest_key.reshape(1, rows),
        active_from.reshape(1, keys),
        cohort.reshape(1, keys),
        day_order(days),
    )


def scale_kernel(scale_ref, raw_ref, out_ref, taken, given, in_sems, out_sems):
    keys, kinds = taken.shape[:2]
    parts = in_sems.shape[0]
    block = keys // parts

    def spot(part):
        return pl.ds(part * block, block)

    def read(part):
        return pltpu.make_async_copy(raw_ref.at[spot(part)], taken.at[spot(part)], in_sems.at[part])

    def write(part):
        return pltpu.make_async_copy(given.at[spot(part)], out_ref.at[spot(part)], out_sems.at[part])

    for part in range(parts):
        read(part).start()
    for part in range(parts):
        read(part).wait()

        def pair(index, carry):
            for local in range(4):
                key = part * block + index * 4 + local
                for w in range(kinds):
                    value = taken[key, w].astype(jnp.float32) * scale_ref[w, key]
                    given[key, w] = value.astype(jnp.bfloat16)
            return carry

        lax.fori_loop(0, block // 4, pair, 0)
        write(part).start()
    for part in range(parts):
        write(part).wait()


def scale(raw, norm_scale):
    hbm = pl.BlockSpec(memory_space=pl.ANY)
    parts = 16
    return pl.pallas_call(
        scale_kernel,
        out_shape=jax.ShapeDtypeStruct(raw.shape, jnp.bfloat16),
        in_specs=[pl.BlockSpec(memory_space=pltpu.SMEM), hbm],
        out_specs=hbm,
        scratch_shapes=[
            pltpu.VMEM(raw.shape, jnp.bfloat16),
            pltpu.VMEM(raw.shape, jnp.bfloat16),
            pltpu.SemaphoreType.DMA((parts,)),
            pltpu.SemaphoreType.DMA((parts,)),
        ],
        compiler_params=pltpu.CompilerParams(vmem_limit_bytes=60 << 20),
    )(norm_scale, raw)


def on_device(partials, dest_key, active_from, cohort, decay_rate):
    key_devs = lax.axis_size("key")
    _, feat_count, day_count = partials.shape
    raw, norm_scale, own = main(partials, dest_key, active_from, cohort, decay_rate, key_devs)
    windowed = scale(raw, norm_scale)
    kinds = len(WINDOWS)
    share = day_count // key_devs
    own = own.reshape(kinds, feat_count * COHORTS // BLOCK, share, BLOCK // COHORTS, COHORTS)
    own = own.transpose(4, 0, 1, 3, 2)
    return (windowed, own.reshape(COHORTS, kinds, feat_count, share))


def solution(mesh):
    placed = (P("key", "feat", None), P("key"), P("key"), P("key"), P(None, "feat"))
    return jax.shard_map(
        on_device,
        mesh=mesh,
        in_specs=placed,
        out_specs=(P("key", None, "feat", None), P(None, None, "feat", "key")),
        check_vma=False,
    )
```
